256 devices in a mesh: blk: 32 (over z, x_hi, core), heads: 8 (over y, x_lo).
Axes of the slice: x: 4 (x_hi: 2, x_lo: 2; x = x_hi * 2 + x_lo), y: 4, z: 8, core: 2. Of those that a mesh axis runs over, the one named last changes fastest.
Arguments:
- queries: bfloat16 [8192, 5120], P('blk', 'heads'), may hold values from -8 to 8
- key_rows: bfloat16 [8192, 5120], P('blk', 'heads'), may hold values from -8 to 8
- value_rows: bfloat16 [8192, 5120], P('blk', 'heads'), may hold values from -12 to 12
- frame_ids: int32 [8192], P('blk'), may hold values from 0 to 7, never falling along the last dimension, each value on 1 to 2048 neighbouring positions
- ctx_keys: bfloat16 [32, 256, 5120], P('blk', None, 'heads'), may hold values from -8 to 8
- ctx_values: bfloat16 [32, 256, 5120], P('blk', None, 'heads'), may hold values from -12 to 12
- owners: int32 [4], replicated, may hold values from 0 to 31, as said below
- ctx_lengths: int32 [4], replicated, may hold values from 1 to 256, 768 in all
- out_weight: bfloat16 [5120, 5120], P('heads'), may hold values from -0.078125 to 0.078125
Outputs:
- projected: bfloat16 [8192, 5120], P('blk', 'heads')
The draws below stay inside these ranges and needn't reach their ends.
Inputs may be any that keep to these rules, and one draw needn't show every extreme that they name: `owners`: 4 distinct slot numbers. `frame_ids`: never falling along the tokens; every frame from 0 to 7 occurs.
All inputs are finite; a program needn't handle non-finite values.
Results may differ from the reference program's by a relative error of at most 0.019.
Values may be sent and summed in bfloat16 or wider, within the bound.
No kernel may reach another device: no remote copies, remote signals or barrier semaphores. Data moves between devices by JAX's collectives and lax.ppermute only.
A program may use at most 192 MiB of HBM per device.

```python
import math
import jax
import jax.numpy as jnp
import numpy as np
from jax import lax

D = 5120
HEADS = 40
DH = 128
CLEN = 256
NCTX = 4
FRAMES = 8
TOKENS = 8192
SLOTS = 32
FRAME_MOST = 2048
CTX_TOTAL = 768
N_BLK = 32


def draw_queries(key, part):
    key = jax.random.fold_in(key, 1)
    base = jnp.clip(1.4 * jax.random.normal(key, (TOKENS, D), jnp.float32), -8.0, 8.0)
    return base.astype(jnp.bfloat16)


def draw_key_rows(key, part):
    key = jax.random.fold_in(key, 2)
    base = jnp.clip(1.4 * jax.random.normal(key, (TOKENS, D), jnp.float32), -8.0, 8.0)
    return base.astype(jnp.bfloat16)


def draw_owners(key, part):
    key = jax.random.fold_in(key, 7)
    middle = jax.random.permutation(key, N_BLK - 2)[:NCTX - 2].astype(jnp.int32) + 1
    values = jnp.concatenate([jnp.array([0, N_BLK - 1], jnp.int32), middle])
    return jax.random.permutation(jax.random.fold_in(key, 1), values).astype(jnp.int32)


def block_levels(rng, shape, pieces, least, high):
    def one(position, blocks):
        steps = jax.random.uniform(jax.random.fold_in(jax.random.fold_in(rng, 6), position), (blocks,), jnp.float32, least / len(pieces), high / len(pieces))
        return jnp.repeat(jnp.exp(steps), shape[position] // blocks).reshape((-1,) + (1,) * (len(shape) - position - 1))

    level = one(*pieces[0])
    for cut in pieces[1:]:
        level = level * one(*cut)
    return level


def length_profile(number_of, total, reach, skew):
    loads = [(1 << 20) // math.isqrt(standing ** skew) + 1 for standing in range(2, number_of + 1)]
    spare, counts = total - reach - (number_of - 1), [1] * (number_of - 1)
    while spare > 0:
        candidates = [i for i in range(number_of - 1) if counts[i] < reach]
        mass, budget = sum([loads[i] for i in candidates]), spare
        for i in candidates:
            extra = min(reach - counts[i], max(1, budget * loads[i] // mass), spare)
            counts[i] = counts[i] + extra
            spare = spare - extra
    return np.array([reach] + counts)


def ragged(own_key, count, total, most, lean):
    if count == 2:
        one = jax.random.randint(own_key, (), max(1, total - most), min(most, total - 1) + 1)
        return jnp.stack([one, total - one])
    lengths = jnp.asarray(length_profile(count, total, most, lean), jnp.int32)
    pairs = (count - 1) // 2
    source_of, sink = lengths[1:1 + 2 * pairs:2], lengths[2:2 + 2 * pairs:2]
    slack = jnp.minimum(source_of - 1, most - sink)
    moved = jax.random.randint(jax.random.fold_in(own_key, 1), (pairs,), 0, 1 << 20) % (slack + 1)
    lengths = lengths.at[1:1 + 2 * pairs:2].set(source_of - moved).at[2:2 + 2 * pairs:2].set(sink + moved)
    return lengths[jax.random.permutation(jax.random.fold_in(own_key, 2), count)]


def gaussian(own_key, extent, width, most, shards=(), kind=jnp.bfloat16):
    loudness = block_levels(own_key, extent, shards, -0.22, 0.18) if shards else 1.0
    values = jax.random.normal(own_key, extent, jnp.float32) * width * loudness
    return jnp.minimum(jnp.maximum(values, -most), most).astype(kind)


def setup_inputs(seed: int = 0) -> dict:
    splits = jax.random.split(jax.random.key(seed), 10)
    queries = draw_queries(jax.random.fold_in(splits[9], 71), 0)
    key_rows = draw_key_rows(jax.random.fold_in(splits[9], 71), 0)
    value_rows = gaussian(splits[2], (TOKENS, D), 3.0, 12.0, ((0, 32), (1, 8)))
    frame_ids = jnp.searchsorted(jnp.cumsum(ragged(splits[3], FRAMES, TOKENS, FRAME_MOST, 1)), jnp.arange(TOKENS), side="right").astype(jnp.int32)
    ctx_keys = gaussian(splits[4], (SLOTS, CLEN, D), 1.4, 8.0, ((0, 32), (2, 8)))
    ctx_values = gaussian(splits[5], (SLOTS, CLEN, D), 3.0, 12.0, ((0, 32), (2, 8)))
    owners = draw_owners(jax.random.fold_in(splits[9], 71), 0)
    ctx_lengths = ragged(splits[7], NCTX, CTX_TOTAL, CLEN, 1).astype(jnp.int32)
    out_weight = gaussian(splits[8], (D, D), D ** -0.5, 0.078125, ((0, 8),))
    return {"queries": queries, "key_rows": key_rows, "value_rows": value_rows, "frame_ids": frame_ids, "ctx_keys": ctx_keys, "ctx_values": ctx_values, "owners": owners, "ctx_lengths": ctx_lengths, "out_weight": out_weight}


def reference(queries, key_rows, value_rows, frame_ids, ctx_keys, ctx_values, owners, ctx_lengths, out_weight):
    scale_value = DH ** -0.5
    chosen_keys = ctx_keys[owners].reshape(NCTX * CLEN, D)
    chosen_values = ctx_values[owners].reshape(NCTX * CLEN, D)
    all_keys = jnp.concatenate([chosen_keys, key_rows], axis=0)
    all_values = jnp.concatenate([chosen_values, value_rows], axis=0)
    positions = jnp.arange(CLEN, dtype=jnp.int32)
    ctx_valid = (positions[None, :] < ctx_lengths[:, None]).reshape(-1)
    key_frames = jnp.concatenate([jnp.full((NCTX * CLEN,), -1, jnp.int32), frame_ids.astype(jnp.int32)])
    key_valid = jnp.concatenate([ctx_valid, jnp.ones((TOKENS,), bool)])
    allowed = (key_frames[None, :] <= frame_ids[:, None]) & key_valid[None, :]

    def head_attention(head_index):
        start_col = head_index * DH
        head_queries = lax.dynamic_slice_in_dim(queries, start_col, DH, 1)
        head_keys = lax.dynamic_slice_in_dim(all_keys, start_col, DH, 1)
        head_values = lax.dynamic_slice_in_dim(all_values, start_col, DH, 1)
        scores = jnp.dot(head_queries, head_keys.T, preferred_element_type=jnp.float32) * scale_value
        scores = jnp.where(allowed, scores, -jnp.inf)
        row_top = jnp.max(scores, axis=1, keepdims=True)
        weights = jnp.exp(scores - row_top)
        totals = jnp.sum(weights, axis=1, keepdims=True)
        mixed = jnp.dot(weights.astype(jnp.bfloat16), head_values, preferred_element_type=jnp.float32) / totals
        return mixed.astype(jnp.bfloat16)

    heads_out = lax.map(head_attention, jnp.arange(HEADS, dtype=jnp.int32))
    attended = jnp.transpose(heads_out, (1, 0, 2)).reshape(TOKENS, D)
    return jnp.dot(attended, out_weight, preferred_element_type=jnp.float32).astype(jnp.bfloat16)
```

```python
import functools
import math

import jax
import jax.numpy as jnp
from jax import lax
from jax.experimental import pallas as pl
from jax.experimental.pallas import tpu as pltpu
from jax.sharding import PartitionSpec as P

DH = 128
LOW = -1e30
MASKED = -3e30
FRAMES = 8


def scaled_exponent():
    return DH ** (-0.5) * math.log2(math.e)


def attention_kernel(
    chunk_count, first, last, with_ctx, head_count, rows, *refs
):
    refs = list(refs)
    ctx_len = refs.pop(0) if with_ctx else None
    query_refs = [refs.pop(0) for _ in range(4)]
    query_marks = [refs.pop(0) for _ in range(4)]
    chunks = []
    for index in range(chunk_count):
        is_ctx = with_ctx and index == chunk_count - 1
        key_ref = refs.pop(0)
        value_ref = refs.pop(0)
        mark_ref = None if is_ctx else refs.pop(0)
        chunks.append((key_ref, value_ref, mark_ref))
    if not first:
        acc_in = refs.pop(0)
        stat_in = refs.pop(0)
    if last:
        keep_out = refs.pop(0)
        send_out = refs.pop(0)
    else:
        acc_out = refs.pop(0)
        stat_out = refs.pop(0)
    limits = refs.pop(0)
    bounds = refs.pop(0)
    if last:
        stats = refs.pop(0)

    head = pl.program_id(0)

    @pl.when(head == 0)
    def _():
        for index, (_, _, mark_ref) in enumerate(chunks):
            if mark_ref is not None:
                key_marks = mark_ref[0:1, 0:rows].astype(jnp.float32)
                below = [
                    jnp.sum((key_marks <= f).astype(jnp.float32), axis=1, keepdims=True)
                    for f in range(FRAMES)
                ]
            for group in range(4):
                if mark_ref is None:
                    limit = jnp.full((1, rows), ctx_len[0].astype(jnp.float32), jnp.float32)
                else:
                    marks = query_marks[group][0:1, :].astype(jnp.float32)
                    limit = jnp.zeros((1, rows), jnp.float32)
                    for f in range(FRAMES):
                        limit = jnp.where(marks == f, below[f], limit)
                limits[index, group * 8 : group * 8 + 1, :] = limit
                bounds[index, group, 0] = jnp.min(limit).astype(jnp.int32)
                bounds[index, group, 1] = jnp.max(limit).astype(jnp.int32)

    factor = scaled_exponent()
    for group in range(4):
        lanes = pl.ds(group * rows, rows)
        if first:
            top = jnp.full((1, rows), LOW, jnp.float32)
            total = jnp.zeros((1, rows), jnp.float32)
            acc_scr = None
        if last:
            acc_ref, stat_ref = acc_in, stat_in
        elif first:
            acc_ref, stat_ref = acc_out, stat_out
            acc_out[:, lanes] = jnp.zeros((DH, rows), jnp.float32)
            stat_out[0:1, lanes] = top
            stat_out[1:2, lanes] = total
        else:
            acc_ref, stat_ref = acc_out, stat_out
            acc_out[:, lanes] = acc_in[:, lanes]
            stat_out[0:2, lanes] = stat_in[0:2, lanes]
        query_block = query_refs[group][...]
        for index, (key_ref, value_ref, _) in enumerate(chunks):

            def update(masked, key_ref=key_ref, value_ref=value_ref, index=index):
                scores = (
                    jnp.dot(key_ref[...], query_block, preferred_element_type=jnp.float32) * factor
                )
                if masked:
                    place = lax.broadcasted_iota(jnp.int32, scores.shape, 0).astype(jnp.float32)
                    limit = limits[index, group * 8 : group * 8 + 1, :]
                    scores = jnp.where(place < limit, scores, MASKED)
                top_old = stat_ref[0:1, lanes]
                top_new = jnp.maximum(top_old, jnp.max(scores, axis=0, keepdims=True))
                weights = jnp.exp2(scores - top_new)
                fade = jnp.exp2(top_old - top_new)
                stat_ref[0:1, lanes] = top_new
                stat_ref[1:2, lanes] = stat_ref[1:2, lanes] * fade + jnp.sum(
                    weights, axis=0, keepdims=True
                )
                acc_ref[:, lanes] = acc_ref[:, lanes] * fade + jnp.dot(
                    value_ref[...],
                    weights.astype(jnp.bfloat16),
                    preferred_element_type=jnp.float32,
                )

            low, high = bounds[index, group, 0], bounds[index, group, 1]
            full = low >= rows

            @pl.when(full)
            def _():
                update(False)

            @pl.when(jnp.logical_and(high > 0, jnp.logical_not(full)))
            def _():
                update(True)

        if last:
            out_ref = keep_out if group < 2 else send_out
            half = pl.ds((group % 2) * rows, rows)
            total = stat_ref[1:2, lanes]
            spot = pl.ds(pl.multiple_of(head * DH, DH), DH)
            out_ref[spot, half] = (acc_ref[:, lanes] * (1.0 / total)).astype(jnp.bfloat16)
            level = stat_ref[0:1, lanes] + jnp.log2(total)
            for part in range(3):
                piece = level.astype(jnp.bfloat16).astype(jnp.float32)
                stats[pl.ds(part * head_count + head, 1), lanes] = piece
                level = level - piece

    if last:

        @pl.when(head == head_count - 1)
        def _():
            feat = head_count * DH
            keep_out[feat : feat + 16, :] = stats[:, 0 : 2 * rows].astype(jnp.bfloat16)
            send_out[feat : feat + 16, :] = stats[:, 2 * rows : 4 * rows].astype(jnp.bfloat16)


def attention_call(queries, chunks, state, ctx_len, last):
    feat = queries[0].shape[0] - 16
    rows = queries[0].shape[1]
    head_count = feat // DH
    first = state is None
    with_ctx = ctx_len is not None
    operands, specs = [], []
    if with_ctx:
        operands.append(ctx_len)
        specs.append(pl.BlockSpec(memory_space=pltpu.SMEM))
    for block in queries:
        operands.append(block)
        specs.append(pl.BlockSpec((DH, rows), lambda h: (h, 0)))
    for block in queries:
        operands.append(block)
        specs.append(pl.BlockSpec((16, rows), lambda h: (feat // 16, 0)))
    for index, (keys, values) in enumerate(chunks):
        operands.append(keys)
        specs.append(pl.BlockSpec((rows, DH), lambda h: (0, h)))
        operands.append(values)
        specs.append(pl.BlockSpec((DH, rows), lambda h: (h, 0)))
        if not (with_ctx and index == len(chunks) - 1):
            operands.append(keys)
            specs.append(pl.BlockSpec((16, feat), lambda h: (rows // 16, 0)))
    aliases = {}
    state_specs = [
        pl.BlockSpec((DH, 4 * rows), lambda h: (h, 0)),
        pl.BlockSpec((8, 4 * rows), lambda h: (h, 0)),
    ]
    if not first:
        if not last:
            aliases = {len(operands): 0, len(operands) + 1: 1}
        operands.extend(state)
        specs.extend(state_specs)
    if last:
        out_shape = [jax.ShapeDtypeStruct((feat + 16, 2 * rows), jnp.bfloat16)] * 2
        out_specs = [pl.BlockSpec((feat + 16, 2 * rows), lambda h: (0, 0))] * 2
    else:
        out_shape = [
            jax.ShapeDtypeStruct((feat, 4 * rows), jnp.float32),
            jax.ShapeDtypeStruct((8 * head_count, 4 * rows), jnp.float32),
        ]
        out_specs = state_specs
    scratch = [
        pltpu.VMEM((len(chunks), 32, rows), jnp.float32),
        pltpu.SMEM((len(chunks), 4, 2), jnp.int32),
    ]
    if last:
        scratch.append(pltpu.VMEM((16, 4 * rows), jnp.float32))
    work = head_count * 4 * rows * rows * len(chunks)
    return pl.pallas_call(
        functools.partial(
            attention_kernel, len(chunks), first, last, with_ctx, head_count, rows
        ),
        grid=(head_count,),
        in_specs=specs,
        out_specs=out_specs,
        out_shape=out_shape,
        scratch_shapes=scratch,
        input_output_aliases=aliases,
        cost_estimate=pl.CostEstimate(
            flops=work * DH * 4, bytes_accessed=8 << 20, transcendentals=work
        ),
        compiler_params=pltpu.CompilerParams(vmem_limit_bytes=48 << 20),
    )(*operands)


def merge_kernel(head_count, turned, a_ref, b_ref, out_ref, *rest):
    feat = head_count * DH
    rows = a_ref.shape[1]
    a_stats = a_ref[feat : feat + 16, :].astype(jnp.float32)
    b_stats = b_ref[feat : feat + 16, :].astype(jnp.float32)
    pieces = [[], [], []]
    for head in range(head_count):
        levels = [
            s[head : head + 1]
            + s[head_count + head : head_count + head + 1]
            + s[2 * head_count + head : 2 * head_count + head + 1]
            for s in (a_stats, b_stats)
        ]
        top = jnp.maximum(levels[0], levels[1])
        a_weight = jnp.exp2(levels[0] - top)
        b_weight = jnp.exp2(levels[1] - top)
        total = a_weight + b_weight
        inverse = 1.0 / total
        span = slice(head * DH, (head + 1) * DH)
        mixed = a_ref[span, :].astype(jnp.float32) * (a_weight * inverse) + b_ref[span, :].astype(
            jnp.float32
        ) * (b_weight * inverse)
        if turned:
            out_ref[:, span] = mixed.T.astype(jnp.bfloat16)
        else:
            half = rows // 2
            out_ref[span, :] = mixed[:, :half].astype(jnp.bfloat16)
            rest[0][span, :] = mixed[:, half:].astype(jnp.bfloat16)
            level = top + jnp.log2(total)
            for part in range(3):
                piece = level.astype(jnp.bfloat16).astype(jnp.float32)
                pieces[part].append(piece)
                level = level - piece
    if not turned:
        stats = jnp.concatenate(
            pieces[0] + pieces[1] + pieces[2] + [jnp.zeros((1, rows), jnp.float32)], axis=0
        ).astype(jnp.bfloat16)
        out_ref[feat : feat + 16, :] = stats[:, :half]
        rest[0][feat : feat + 16, :] = stats[:, half:]


def merge_call(a, b, turned):
    feat = a.shape[0] - 16
    rows = a.shape[1]
    if turned:
        out_shape = jax.ShapeDtypeStruct((rows, feat), jnp.bfloat16)
        out_specs = pl.BlockSpec(memory_space=pltpu.VMEM)
    else:
        out_shape = [jax.ShapeDtypeStruct((feat + 16, rows // 2), jnp.bfloat16)] * 2
        out_specs = [pl.BlockSpec(memory_space=pltpu.VMEM)] * 2
    return pl.pallas_call(
        functools.partial(merge_kernel, feat // DH, turned),
        in_specs=[pl.BlockSpec(memory_space=pltpu.VMEM)] * 2,
        out_specs=out_specs,
        out_shape=out_shape,
        compiler_params=pltpu.CompilerParams(vmem_limit_bytes=32 << 20),
    )(a, b)


def shards(
    queries, key_rows, value_rows, frame_ids, ctx_keys, ctx_values, owners, ctx_lengths, out_weight
):
    rows, feat = queries.shape
    blk_count = lax.axis_size("blk")
    head_devices = lax.axis_size("heads")
    plane = 4
    depth = blk_count // plane
    me = lax.axis_index("blk")
    kind = lax.rem(me, plane)
    columns = [[c + plane * z for z in range(depth)] for c in range(plane)]
    planes = [[plane * z + c for c in range(plane)] for z in range(depth)]
    swap_core = [(i, i ^ 1) for i in range(blk_count)]
    swap_x = [(i, i ^ 2) for i in range(blk_count)]
    forward = [(i, (i + plane) % blk_count) for i in range(blk_count)]
    backward = [(i, (i - plane) % blk_count) for i in range(blk_count)]

    marks = jnp.zeros((16, feat), jnp.bfloat16)
    marks = marks.at[0, :rows].set(frame_ids.astype(jnp.bfloat16))
    key_own = jnp.concatenate([key_rows, marks], axis=0)
    value_own = value_rows.T
    query_own = jnp.concatenate([queries.T, marks[:, :rows]], axis=0)

    slot = jnp.concatenate([ctx_keys[0], ctx_values[0]], axis=1)
    part = slot.shape[0] // depth
    pieces = lax.all_to_all(
        slot.reshape(depth, part, 2 * feat), "blk", 0, 0, axis_index_groups=columns
    )
    picked = jnp.take(pieces, owners // plane, axis=0)
    offered = lax.all_to_all(picked, "blk", 0, 0, axis_index_groups=planes)
    my_owner = lax.dynamic_index_in_dim(owners, kind, 0, False)
    piece = lax.dynamic_index_in_dim(offered, lax.rem(my_owner, plane), 0, False)
    ctx = lax.all_gather(piece, "blk", axis=0, tiled=True, axis_index_groups=columns)
    ctx_key = ctx[:, :feat]
    ctx_value = ctx[:, feat:].T
    ctx_len = lax.dynamic_index_in_dim(ctx_lengths, kind, 0, True)

    query_x = lax.ppermute(query_own, "blk", swap_x)
    query_core = lax.ppermute(query_own, "blk", swap_core)
    query_both = lax.ppermute(query_x, "blk", swap_core)
    query_groups = [query_own, query_x, query_core, query_both]

    state = attention_call(query_groups, [(key_own, value_own)], None, None, False)
    ahead = behind = (key_own, value_own)
    for _ in range(depth // 2 - 1):
        ahead = tuple(lax.ppermute(item, "blk", forward) for item in ahead)
        behind = tuple(lax.ppermute(item, "blk", backward) for item in behind)
        state = attention_call(query_groups, [ahead, behind], state, None, False)
    farthest = (
        lax.ppermute(ahead[0], "blk", forward),
        lax.ppermute(behind[1], "blk", backward),
    )
    keep, send = attention_call(
        query_groups, [farthest, (ctx_key, ctx_value)], state, ctx_len, True
    )
    received = lax.ppermute(send, "blk", swap_core)
    own, other = merge_call(keep, received, False)
    received = lax.ppermute(other, "blk", swap_x)
    attended = merge_call(own, received, True)

    pair = 2
    ring = head_devices // pair
    head_me = lax.axis_index("heads")
    y_groups = [[pair * y + x for y in range(ring)] for x in range(pair)]
    weight = lax.all_to_all(
        out_weight, "heads", 1, 0, axis_index_groups=y_groups, tiled=True
    ).reshape(ring, feat, pair * feat)
    y_me = head_me // pair
    x_me = lax.rem(head_me, pair)
    total_mine = total_other = 0.0
    for step in range(ring):
        block = attended
        if step:
            block = lax.ppermute(
                attended,
                "heads",
                [(i, (i + pair * step) % head_devices) for i in range(head_devices)],
            )
        source = lax.rem(y_me - step + ring, ring)
        slab = lax.dynamic_index_in_dim(weight, source, 0, False)
        mine = lax.dynamic_slice_in_dim(slab, x_me * feat, feat, 1)
        other = lax.dynamic_slice_in_dim(slab, (1 - x_me) * feat, feat, 1)
        total_other += jnp.dot(block, other, preferred_element_type=jnp.float32)
        total_mine += jnp.dot(block, mine, preferred_element_type=jnp.float32)
    received = lax.ppermute(
        total_other.astype(jnp.bfloat16), "heads", [(i, i ^ 1) for i in range(head_devices)]
    )
    return (total_mine + received.astype(jnp.float32)).astype(jnp.bfloat16)


def solution(mesh):
    return jax.shard_map(
        shards,
        mesh=mesh,
        in_specs=(
            P("blk", "heads"),
            P("blk", "heads"),
            P("blk", "heads"),
            P("blk"),
            P("blk", None, "heads"),
            P("blk", None, "heads"),
            P(),
            P(),
            P("heads", None),
        ),
        out_specs=P("blk", "heads"),
        check_vma=False,
    )
```

```python
import functools
import math

import jax
import jax.numpy as jnp
from jax import lax
from jax.experimental import pallas as pl
from jax.experimental.pallas import tpu as pltpu
from jax.sharding import PartitionSpec as P

DH = 128
LOW = -1e30
MASKED = -3e30
FRAMES = 8
VMEM = 60 << 20


def scaled_exponent():
    return DH ** (-0.5) * math.log2(math.e)


def attention_kernel(chunk_count, first, last, with_ctx, head_count, rows, *refs):
    refs = list(refs)
    ctx_info = refs.pop(0) if with_ctx else None
    query_ref = refs.pop(0)
    query_marks = refs.pop(0)
    chunks = []
    for index in range(chunk_count):
        is_ctx = with_ctx and index == chunk_count - 1
        key_ref = refs.pop(0)
        value_ref = refs.pop(0)
        mark_ref = None if is_ctx else refs.pop(0)
        chunks.append((key_ref, value_ref, mark_ref))
    if not first:
        acc_in = refs.pop(0)
        stat_in = refs.pop(0)
    if last:
        keep_out = refs.pop(0)
        send_out = refs.pop(0)
    else:
        acc_out = refs.pop(0)
        stat_out = refs.pop(0)
        token_out = refs.pop(0)
    limits = refs.pop(0)
    bounds = refs.pop(0)
    if last:
        stats = refs.pop(0)
        levels = refs.pop(0)

    head = pl.program_id(0)
    lane = 128
    factor = scaled_exponent()

    @pl.when(head == 0)
    def _():
        for index, (_, _, mark_ref) in enumerate(chunks):
            if mark_ref is None:
                live = ctx_info[4 + jnp.bitwise_and(ctx_info[8], 3)]
                limits[index, 0:1, :] = jnp.full(
                    (1, 4 * rows), live.astype(jnp.float32), jnp.float32
                )
                bounds[index] = jnp.int32(1)
                continue
            frame = lax.broadcasted_iota(jnp.int32, (FRAMES, rows), 0).astype(jnp.float32)
            key_marks = mark_ref[0:1, 0:rows].astype(jnp.float32)
            below = jnp.sum((key_marks <= frame).astype(jnp.float32), axis=1, keepdims=True)
            frame = lax.broadcasted_iota(jnp.int32, (FRAMES, 4 * rows), 0).astype(jnp.float32)
            marks = query_marks[0:1, :].astype(jnp.float32)
            most = jnp.sum(jnp.where(marks == frame, below, 0.0), axis=0, keepdims=True)
            limits[index, 0:1, :] = most
            bounds[index] = jnp.max(most).astype(jnp.int32)

    def update():
        row = lax.broadcasted_iota(jnp.int32, (rows, lane), 0)
        places = [row.astype(jnp.float32)] * chunk_count
        if with_ctx:
            start = (lax.shift_right_logical(ctx_info[8], 2) + 5) * (rows // 8)
            places[-1] = jnp.bitwise_and(row + start, rows - 1).astype(jnp.float32)
        turned = [value_ref[...].T for _, value_ref, _ in chunks]
        for tile in range(4 * rows // lane):
            spot = slice(tile * lane, (tile + 1) * lane)
            query = query_ref[:, spot]
            if first:
                top = jnp.full((1, lane), LOW, jnp.float32)
                total = jnp.zeros((1, lane), jnp.float32)
                acc = jnp.zeros((DH, lane), jnp.float32)
            else:
                top, total, acc = stat_in[0:1, spot], stat_in[1:2, spot], acc_in[:, spot]
            for index, (key_ref, _, _) in enumerate(chunks):
                scores = jnp.dot(key_ref[...], query, preferred_element_type=jnp.float32)
                scores = jnp.where(places[index] < limits[index, 0:1, spot], scores, MASKED)
                top_new = jnp.maximum(top, jnp.max(scores, axis=0, keepdims=True))
                weights = jnp.exp2((scores - top_new) * factor)
                fade = jnp.exp2((top - top_new) * factor)
                total = total * fade + jnp.sum(weights, axis=0, keepdims=True)
                acc = acc * fade + jnp.dot(
                    turned[index],
                    weights.astype(jnp.bfloat16),
                    preferred_element_type=jnp.float32,
                )
                top = top_new
            if not last:
                stat_out[0:1, spot] = top
                stat_out[1:2, spot] = total
                acc_out[:, spot] = acc
                continue
            out_ref, begin = (keep_out, 0) if tile * lane < 2 * rows else (send_out, 2 * rows)
            out_spot = slice(tile * lane - begin, (tile + 1) * lane - begin)
            out_ref[pl.ds(pl.multiple_of(head * DH, DH), DH), out_spot] = (
                acc * (1.0 / total)
            ).astype(jnp.bfloat16)
            levels[0:1, spot] = top * factor + jnp.log2(total)
        if last:
            level = levels[0:1, :]
            for part in range(3):
                piece = level.astype(jnp.bfloat16).astype(jnp.float32)
                stats[pl.ds(part * head_count + head, 1), :] = piece
                level = level - piece

    if first or last:
        update()
    else:
        seen = functools.reduce(jnp.maximum, [bounds[index] for index in range(chunk_count)]) > 0

        @pl.when(seen)
        def _():
            update()

        @pl.when(jnp.logical_not(seen))
        def _():
            acc_out[...] = acc_in[...]
            stat_out[0:2, :] = stat_in[0:2, :]

    if not last:
        token_out[...] = jnp.zeros_like(token_out)
    else:

        @pl.when(head == head_count - 1)
        def _():
            feat = head_count * DH
            keep_out[feat : feat + 16, :] = stats[:, 0 : 2 * rows].astype(jnp.bfloat16)
            send_out[feat : feat + 16, :] = stats[:, 2 * rows : 4 * rows].astype(jnp.bfloat16)


def attention_call(queries, chunks, state, ctx_info, last):
    feat = queries.shape[0] - 16
    rows = queries.shape[1] // 4
    head_count = feat // DH
    first = state is None
    with_ctx = ctx_info is not None
    operands, specs = [], []
    if with_ctx:
        operands.append(ctx_info)
        specs.append(pl.BlockSpec(memory_space=pltpu.SMEM))
    operands += [queries, queries]
    specs.append(pl.BlockSpec((DH, 4 * rows), lambda h: (h, 0)))
    specs.append(pl.BlockSpec((16, 4 * rows), lambda h: (feat // 16, 0)))
    for index, chunk in enumerate(chunks):
        keys, values = chunk if isinstance(chunk, tuple) else (chunk, chunk)
        first_value = values.shape[1] // DH - head_count
        operands += [keys, values]
        specs.append(pl.BlockSpec((rows, DH), lambda h: (0, h)))
        specs.append(pl.BlockSpec((rows, DH), lambda h, base=first_value: (0, base + h)))
        if not (with_ctx and index == len(chunks) - 1):
            operands.append(keys)
            specs.append(pl.BlockSpec((16, rows), lambda h: (rows // 16, 0)))
    aliases = {}
    state_specs = [
        pl.BlockSpec((DH, 4 * rows), lambda h: (h, 0)),
        pl.BlockSpec((8, 4 * rows), lambda h: (h, 0)),
    ]
    if not first:
        if not last:
            aliases = {len(operands): 0, len(operands) + 1: 1}
        operands.extend(state)
        specs.extend(state_specs)
    if last:
        out_shape = [jax.ShapeDtypeStruct((feat + 16, 2 * rows), jnp.bfloat16)] * 2
        out_specs = [pl.BlockSpec((feat + 16, 2 * rows), lambda h: (0, 0))] * 2
    else:
        out_shape = [
            jax.ShapeDtypeStruct((feat, 4 * rows), jnp.float32),
            jax.ShapeDtypeStruct((8 * head_count, 4 * rows), jnp.float32),
            jax.ShapeDtypeStruct((8, 128), jnp.float32),
        ]
        out_specs = state_specs + [pl.BlockSpec((8, 128), lambda h: (0, 0))]
    scratch = [
        pltpu.VMEM((len(chunks), 8, 4 * rows), jnp.float32),
        pltpu.SMEM((len(chunks),), jnp.int32),
    ]
    if last:
        scratch += [
            pltpu.VMEM((16, 4 * rows), jnp.float32),
            pltpu.VMEM((8, 4 * rows), jnp.float32),
        ]
    return pl.pallas_call(
        functools.partial(
            attention_kernel, len(chunks), first, last, with_ctx, head_count, rows
        ),
        grid=(head_count,),
        in_specs=specs,
        out_specs=out_specs,
        out_shape=out_shape,
        scratch_shapes=scratch,
        input_output_aliases=aliases,
        cost_estimate=pl.CostEstimate(
            flops=len(chunks) * 6 * 10**9, bytes_accessed=8 << 20, transcendentals=0
        ),
        compiler_params=pltpu.CompilerParams(vmem_limit_bytes=VMEM),
        name="attend",
    )(*operands)


def merge_kernel(head_count, turned, a_ref, b_ref, out_ref, *rest):
    feat = head_count * DH
    rows = a_ref.shape[1]
    a_stats = a_ref[feat : feat + 16, :].astype(jnp.float32)
    b_stats = b_ref[feat : feat + 16, :].astype(jnp.float32)
    pieces = [[], [], []]
    for head in range(head_count):
        levels = [
            s[head : head + 1]
            + s[head_count + head : head_count + head + 1]
            + s[2 * head_count + head : 2 * head_count + head + 1]
            for s in (a_stats, b_stats)
        ]
        top = jnp.maximum(levels[0], levels[1])
        a_weight = jnp.exp2(levels[0] - top)
        b_weight = jnp.exp2(levels[1] - top)
        total = a_weight + b_weight
        inverse = 1.0 / total
        span = slice(head * DH, (head + 1) * DH)
        mixed = a_ref[span, :].astype(jnp.float32) * (a_weight * inverse) + b_ref[span, :].astype(
            jnp.float32
        ) * (b_weight * inverse)
        if turned:
            out_ref[:, span] = mixed.T.astype(jnp.bfloat16)
        else:
            half = rows // 2
            out_ref[span, :] = mixed[:, :half].astype(jnp.bfloat16)
            rest[0][span, :] = mixed[:, half:].astype(jnp.bfloat16)
            level = top + jnp.log2(total)
            for part in range(3):
                piece = level.astype(jnp.bfloat16).astype(jnp.float32)
                pieces[part].append(piece)
                level = level - piece
    if not turned:
        stats = jnp.concatenate(
            pieces[0] + pieces[1] + pieces[2] + [jnp.zeros((1, rows), jnp.float32)], axis=0
        ).astype(jnp.bfloat16)
        out_ref[feat : feat + 16, :] = stats[:, :half]
        rest[0][feat : feat + 16, :] = stats[:, half:]


def merge_call(a, b, turned):
    feat = a.shape[0] - 16
    rows = a.shape[1]
    if turned:
        out_shape = jax.ShapeDtypeStruct((rows, feat), jnp.bfloat16)
        out_specs = pl.BlockSpec(memory_space=pltpu.VMEM)
    else:
        out_shape = [jax.ShapeDtypeStruct((feat + 16, rows // 2), jnp.bfloat16)] * 2
        out_specs = [pl.BlockSpec(memory_space=pltpu.VMEM)] * 2
    return pl.pallas_call(
        functools.partial(merge_kernel, feat // DH, turned),
        in_specs=[pl.BlockSpec(memory_space=pltpu.VMEM)] * 2,
        out_specs=out_specs,
        out_shape=out_shape,
        compiler_params=pltpu.CompilerParams(vmem_limit_bytes=VMEM),
        cost_estimate=pl.CostEstimate(flops=0, bytes_accessed=6 << 20, transcendentals=0),
        name="merge",
    )(a, b)


def columns_kernel(info, in_ref, out_ref):
    out_ref[0] = in_ref[...]


def column_blocks(weight, info, width, ring):
    rows = weight.shape[0]

    def place(j, info):
        target = jnp.bitwise_and(lax.shift_right_logical(info[9], 1) + j, ring - 1)
        half = jnp.bitwise_xor(jnp.bitwise_and(info[8], 1), lax.shift_right_logical(j, 2))
        return (0, 2 * target + half)

    return pl.pallas_call(
        columns_kernel,
        grid_spec=pltpu.PrefetchScalarGridSpec(
            num_scalar_prefetch=1,
            grid=(ring + 1,),
            in_specs=[pl.BlockSpec((rows, width), place)],
            out_specs=pl.BlockSpec((1, rows, width), lambda j, info: (j, 0, 0)),
        ),
        out_shape=jax.ShapeDtypeStruct((ring + 1, rows, width), weight.dtype),
        compiler_params=pltpu.CompilerParams(vmem_limit_bytes=VMEM),
        cost_estimate=pl.CostEstimate(
            flops=0, bytes_accessed=4 * (ring + 1) * rows * width, transcendentals=0
        ),
        name="columns",
    )(info, weight)


def offer_kernel(info, in_ref, *out_refs):
    for mask, out_ref in enumerate(out_refs):
        owner = info[jnp.bitwise_xor(jnp.bitwise_and(info[8], 3), mask)]
        out_ref[...] = in_ref[lax.shift_right_logical(owner, 2)]


def offer_pieces(pieces, info):
    return pl.pallas_call(
        offer_kernel,
        in_specs=[
            pl.BlockSpec(memory_space=pltpu.SMEM),
            pl.BlockSpec(memory_space=pltpu.VMEM),
        ],
        out_specs=[pl.BlockSpec(memory_space=pltpu.VMEM)] * 4,
        out_shape=[jax.ShapeDtypeStruct(pieces.shape[1:], pieces.dtype)] * 4,
        compiler_params=pltpu.CompilerParams(vmem_limit_bytes=VMEM),
        name="offer",
    )(info, pieces)


def choose_kernel(info, *refs):
    kind = jnp.bitwise_and(info[8], 3)
    source = jnp.bitwise_xor(jnp.bitwise_and(info[kind], 3), kind)
    out_ref = refs[-1]
    for mask, in_ref in enumerate(refs[:-1]):

        @pl.when(source == mask)
        def _(in_ref=in_ref):
            out_ref[...] = in_ref[...]


def choose_piece(offers, info):
    return pl.pallas_call(
        choose_kernel,
        in_specs=[pl.BlockSpec(memory_space=pltpu.SMEM)]
        + [pl.BlockSpec(memory_space=pltpu.VMEM)] * len(offers),
        out_specs=pl.BlockSpec(memory_space=pltpu.VMEM),
        out_shape=jax.ShapeDtypeStruct(offers[0].shape, offers[0].dtype),
        compiler_params=pltpu.CompilerParams(vmem_limit_bytes=VMEM),
        name="choose",
    )(info, *offers)


def shards(
    queries, key_rows, value_rows, frame_ids, ctx_keys, ctx_values, owners, ctx_lengths, out_weight
):
    rows, feat = queries.shape
    blk_count = lax.axis_size("blk")
    head_devices = lax.axis_size("heads")
    plane, pair = 4, 2
    depth, ring_y = blk_count // plane, head_devices // pair
    me = lax.axis_index("blk")
    head_me = lax.axis_index("heads")
    info = jnp.concatenate([owners, ctx_lengths, me[None], head_me[None]]).astype(jnp.int32)
    columns = [[c + plane * z for z in range(depth)] for c in range(plane)]

    def shift(item, distance):
        steps = [(i, (i + plane * distance) % blk_count) for i in range(blk_count)]
        return lax.ppermute(item, "blk", steps)

    def swap(item, mask):
        return lax.ppermute(item, "blk", [(i, i ^ mask) for i in range(blk_count)])

    def shift_y(item, step):
        steps = [(i, (i + pair * step) % head_devices) for i in range(head_devices)]
        return lax.ppermute(item, "heads", steps)

    marks = jnp.pad(frame_ids.astype(jnp.bfloat16)[None], ((0, 15), (0, 2 * feat - rows)))
    own = jnp.concatenate([jnp.concatenate([key_rows, value_rows], axis=1), marks], axis=0)
    query_own = jnp.concatenate([queries.T, marks[:, :rows]], axis=0)
    part = ctx_keys.shape[1] // depth
    slot = jnp.concatenate([ctx_keys[0], ctx_values[0]], axis=1).reshape(depth, part, 2 * feat)

    ahead, behind = shift(own, 1), shift(own, -1)
    query_x, query_core, query_both = swap(query_own, 2), swap(query_own, 1), swap(query_own, 3)
    pieces = lax.all_to_all(slot, "blk", 0, 0, axis_index_groups=columns)
    slabs = column_blocks(out_weight, info, feat, ring_y)
    query_plane = jnp.concatenate([query_own, query_x, query_core, query_both], axis=1)
    offers = list(offer_pieces(pieces, info))

    *state, _ = attention_call(query_plane, [own, ahead, behind], None, None, False)
    ahead, behind = shift(ahead, 1), shift(behind, -1)
    offers = offers[:1] + [swap(offers[mask], mask) for mask in range(1, plane)]
    piece = choose_piece(offers, info)

    *state, _ = attention_call(query_plane, [ahead, behind], state, None, False)
    ahead, behind = shift(ahead, 1), shift(behind, -1)
    ctx = {0: piece}
    for distance in (1, -1, 2, -2):
        ctx[distance] = shift(piece, distance)
    slab_near = shift_y(slabs[1], 1)
    slab_back = shift_y(slabs[ring_y - 1], ring_y - 1)
    ahead, behind, slab_near, slab_back = lax.optimization_barrier(
        (ahead, behind, slab_near, slab_back)
    )

    far = ahead[:, :feat], behind[:rows, feat:]
    *state, _ = attention_call(query_plane, [ahead, behind], state, None, False)
    far = shift(far[0], 1), shift(far[1], -1)
    ctx[3] = shift(ctx[2], 1)
    ctx[4] = shift(ctx[2], 2)
    ctx[-3] = shift(ctx[-2], -1)
    slab_far = shift_y(slabs[2], 2)
    ctx = jnp.concatenate([ctx[distance] for distance in (3, 2, 1, 0, -1, -2, -3, 4)], axis=0)
    own_slabs = [slabs[0], slab_near, slab_far, slab_back]
    core_slabs = [slabs[ring_y], swap(slab_near, 1), None, swap(slab_back, 1)]
    ctx, slab_far, *_ = lax.optimization_barrier((ctx, slab_far, core_slabs[1], core_slabs[3]))
    core_slabs[2] = swap(slab_far, 1)
    keep, send = attention_call(query_plane, [far, ctx], state, info, True)
    keep, send, core_slabs[2] = lax.optimization_barrier((keep, send, core_slabs[2]))
    received = swap(send, 1)
    own, other = merge_call(keep, received, False)
    received = swap(other, 2)
    attended = merge_call(own, received, True)

    def dots(block, step):
        return [
            jnp.dot(block, item[step], preferred_element_type=jnp.float32)
            for item in (own_slabs, core_slabs)
        ]

    total = dots(attended, 0)
    block_near, block_back = shift_y(attended, 1), shift_y(attended, ring_y - 1)
    block_far = shift_y(attended, 2)
    added = [dots(block_near, 1), dots(block_back, ring_y - 1)]
    added.append(dots(block_far, 2))
    total = [sum(items) for items in zip(total, *added)]
    same = jnp.bitwise_and(jnp.bitwise_xor(me, head_me), 1) == 0
    mine = jnp.where(same, total[0], total[1])
    other = jnp.where(same, total[1], total[0])
    received = lax.ppermute(
        other.astype(jnp.bfloat16), "heads", [(i, i ^ 1) for i in range(head_devices)]
    )
    return (mine + received.astype(jnp.float32)).astype(jnp.bfloat16)


def solution(mesh):
    return jax.shard_map(
        shards,
        mesh=mesh,
        in_specs=(
            P("blk", "heads"),
            P("blk", "heads"),
            P("blk", "heads"),
            P("blk"),
            P("blk", None, "heads"),
            P("blk", None, "heads"),
            P(),
            P(),
            P("heads", None),
        ),
        out_specs=P("blk", "heads"),
        check_vma=False,
    )
```

```python
import functools
import math

import jax
import jax.numpy as jnp
from jax import lax
from jax.experimental import pallas as pl
from jax.experimental.pallas import tpu as pltpu
from jax.sharding import PartitionSpec as P

DH = 128
LOW = -1e30
MASKED = -3e30
FRAMES = 8
VMEM = 60 << 20


def scaled_exponent():
    return DH ** (-0.5) * math.log2(math.e)


def attention_kernel(layout, first, last, with_ctx, head_count, rows, *refs):
    refs = list(refs)
    ctx_info = refs.pop(0) if with_ctx else None
    refs.pop(0)
    query_ref = refs.pop(0)
    query_marks = refs.pop(0)
    chunks = []
    for segments, marked in layout:
        keys = [(refs.pop(0), refs.pop(0), begin, count) for begin, count in segments]
        chunks.append((keys, refs.pop(0) if marked else None))
    chunk_count = len(chunks)
    if not first:
        acc_in = refs.pop(0)
        stat_in = refs.pop(0)
    if last:
        keep_out = refs.pop(0)
        send_out = refs.pop(0)
    else:
        acc_out = refs.pop(0)
        stat_out = refs.pop(0)
        token_out = refs.pop(0)
    limits = refs.pop(0)
    bounds = refs.pop(0)
    if last:
        stats = refs.pop(0)
        levels = refs.pop(0)

    head = pl.program_id(0)
    lane = 128
    factor = scaled_exponent()

    @pl.when(head == 0)
    def _():
        for index, (_, mark_ref) in enumerate(chunks):
            if mark_ref is None:
                live = ctx_info[4 + jnp.bitwise_and(ctx_info[8], 3)]
                limits[index, 0:1, :] = jnp.full(
                    (1, 4 * rows), live.astype(jnp.float32), jnp.float32
                )
                bounds[index] = jnp.int32(1)
                continue
            frame = lax.broadcasted_iota(jnp.int32, (FRAMES, rows), 0).astype(jnp.float32)
            key_marks = mark_ref[0:1, 0:rows].astype(jnp.float32)
            below = jnp.sum((key_marks <= frame).astype(jnp.float32), axis=1, keepdims=True)
            frame = lax.broadcasted_iota(jnp.int32, (FRAMES, 4 * rows), 0).astype(jnp.float32)
            marks = query_marks[0:1, :].astype(jnp.float32)
            most = jnp.sum(jnp.where(marks == frame, below, 0.0), axis=0, keepdims=True)
            limits[index, 0:1, :] = most
            bounds[index] = jnp.max(most).astype(jnp.int32)

    def update():
        row = lax.broadcasted_iota(jnp.int32, (rows, lane), 0)
        places = [row.astype(jnp.float32)] * chunk_count
        if with_ctx:
            start = (lax.shift_right_logical(ctx_info[8], 2) + 5) * (rows // 8)
            places[-1] = jnp.bitwise_and(row + start, rows - 1).astype(jnp.float32)
        keys = [
            jnp.concatenate([ref[begin : begin + count] for ref, _, begin, count in segments])
            for segments, _ in chunks
        ]
        turned = [
            jnp.concatenate([ref[begin : begin + count] for _, ref, begin, count in segments]).T
            for segments, _ in chunks
        ]
        for tile in range(4 * rows // lane):
            spot = slice(tile * lane, (tile + 1) * lane)
            query = query_ref[:, spot]
            if first:
                top = jnp.full((1, lane), LOW, jnp.float32)
                total = jnp.zeros((1, lane), jnp.float32)
                acc = jnp.zeros((DH, lane), jnp.float32)
            else:
                top, total, acc = stat_in[0:1, spot], stat_in[1:2, spot], acc_in[:, spot]
            for index in range(chunk_count):
                scores = jnp.dot(keys[index], query, preferred_element_type=jnp.float32)
                scores = jnp.where(places[index] < limits[index, 0:1, spot], scores, MASKED)
                top_new = jnp.maximum(top, jnp.max(scores, axis=0, keepdims=True))
                weights = jnp.exp2((scores - top_new) * factor)
                fade = jnp.exp2((top - top_new) * factor)
                total = total * fade + jnp.sum(weights, axis=0, keepdims=True)
                acc = acc * fade + jnp.dot(
                    turned[index],
                    weights.astype(jnp.bfloat16),
                    preferred_element_type=jnp.float32,
                )
                top = top_new
            if not last:
                stat_out[0:1, spot] = top
                stat_out[1:2, spot] = total
                acc_out[:, spot] = acc
                continue
            out_ref, begin = (keep_out, 0) if tile * lane < 2 * rows else (send_out, 2 * rows)
            out_spot = slice(tile * lane - begin, (tile + 1) * lane - begin)
            out_ref[pl.ds(pl.multiple_of(head * DH, DH), DH), out_spot] = (
                acc * (1.0 / total)
            ).astype(jnp.bfloat16)
            levels[0:1, spot] = top * factor + jnp.log2(total)
        if last:
            level = levels[0:1, :]
            for part in range(3):
                piece = level.astype(jnp.bfloat16).astype(jnp.float32)
                stats[pl.ds(part * head_count + head, 1), :] = piece
                level = level - piece

    if first or last:
        update()
    else:
        seen = functools.reduce(jnp.maximum, [bounds[index] for index in range(chunk_count)]) > 0

        @pl.when(seen)
        def _():
            update()

        @pl.when(jnp.logical_not(seen))
        def _():
            acc_out[...] = acc_in[...]
            stat_out[0:2, :] = stat_in[0:2, :]

    if not last:
        token_out[...] = jnp.zeros_like(token_out)
    else:

        @pl.when(head == head_count - 1)
        def _():
            feat = head_count * DH
            keep_out[feat : feat + 16, :] = stats[:, 0 : 2 * rows].astype(jnp.bfloat16)
            send_out[feat : feat + 16, :] = stats[:, 2 * rows : 4 * rows].astype(jnp.bfloat16)


def attention_call(queries, chunks, state, ctx_info, last, token):
    feat = queries.shape[0] - 16
    rows = queries.shape[1] // 4
    head_count = feat // DH
    first = state is None
    with_ctx = ctx_info is not None
    operands, specs = [], []
    if with_ctx:
        operands.append(ctx_info)
        specs.append(pl.BlockSpec(memory_space=pltpu.SMEM))
    operands += [token, queries, queries]
    specs.append(pl.BlockSpec(memory_space=pl.ANY))
    specs.append(pl.BlockSpec((DH, 4 * rows), lambda h: (h, 0)))
    specs.append(pl.BlockSpec((16, 4 * rows), lambda h: (feat // 16, 0)))
    layout = []
    for segments, marks in chunks:
        places = []
        for array, begin, count in segments:
            block, wanted = 0, count
            if begin % count == 0:
                block, begin = begin // count, 0
            else:
                count = array.shape[0]
            operands += [array, array]
            specs.append(pl.BlockSpec((count, DH), lambda h, at=block: (at, h)))
            specs.append(pl.BlockSpec((count, DH), lambda h, at=block: (at, head_count + h)))
            places.append((begin, wanted))
        layout.append((tuple(places), marks is not None))
        if marks is not None:
            operands.append(marks)
            specs.append(
                pl.BlockSpec((16, rows), lambda h, at=marks.shape[0] // 16 - 1: (at, 0))
            )
    aliases = {}
    state_specs = [
        pl.BlockSpec((DH, 4 * rows), lambda h: (h, 0)),
        pl.BlockSpec((8, 4 * rows), lambda h: (h, 0)),
    ]
    if not first:
        if not last:
            aliases = {len(operands): 0, len(operands) + 1: 1}
        operands.extend(state)
        specs.extend(state_specs)
    if last:
        out_shape = [jax.ShapeDtypeStruct((feat + 16, 2 * rows), jnp.bfloat16)] * 2
        out_specs = [pl.BlockSpec((feat + 16, 2 * rows), lambda h: (0, 0))] * 2
    else:
        out_shape = [
            jax.ShapeDtypeStruct((feat, 4 * rows), jnp.float32),
            jax.ShapeDtypeStruct((8 * head_count, 4 * rows), jnp.float32),
            jax.ShapeDtypeStruct((8, 128), jnp.float32),
        ]
        out_specs = state_specs + [pl.BlockSpec((8, 128), lambda h: (0, 0))]
    scratch = [
        pltpu.VMEM((len(chunks), 8, 4 * rows), jnp.float32),
        pltpu.SMEM((len(chunks),), jnp.int32),
    ]
    if last:
        scratch += [
            pltpu.VMEM((16, 4 * rows), jnp.float32),
            pltpu.VMEM((8, 4 * rows), jnp.float32),
        ]
    return pl.pallas_call(
        functools.partial(
            attention_kernel, layout, first, last, with_ctx, head_count, rows
        ),
        grid=(head_count,),
        in_specs=specs,
        out_specs=out_specs,
        out_shape=out_shape,
        scratch_shapes=scratch,
        input_output_aliases=aliases,
        cost_estimate=pl.CostEstimate(
            flops=len(chunks) * 6 * 10**9, bytes_accessed=8 << 20, transcendentals=0
        ),
        compiler_params=pltpu.CompilerParams(vmem_limit_bytes=VMEM),
        name="attend",
    )(*operands)


def merge_kernel(head_count, turned, a_ref, b_ref, out_ref, *rest):
    feat = head_count * DH
    rows = a_ref.shape[1]
    a_stats = a_ref[feat : feat + 16, :].astype(jnp.float32)
    b_stats = b_ref[feat : feat + 16, :].astype(jnp.float32)
    pieces = [[], [], []]
    for head in range(head_count):
        levels = [
            s[head : head + 1]
            + s[head_count + head : head_count + head + 1]
            + s[2 * head_count + head : 2 * head_count + head + 1]
            for s in (a_stats, b_stats)
        ]
        top = jnp.maximum(levels[0], levels[1])
        a_weight = jnp.exp2(levels[0] - top)
        b_weight = jnp.exp2(levels[1] - top)
        total = a_weight + b_weight
        inverse = 1.0 / total
        span = slice(head * DH, (head + 1) * DH)
        mixed = a_ref[span, :].astype(jnp.float32) * (a_weight * inverse) + b_ref[span, :].astype(
            jnp.float32
        ) * (b_weight * inverse)
        if turned:
            out_ref[:, span] = mixed.T.astype(jnp.bfloat16)
        else:
            half = rows // 2
            out_ref[span, :] = mixed[:, :half].astype(jnp.bfloat16)
            rest[0][span, :] = mixed[:, half:].astype(jnp.bfloat16)
            level = top + jnp.log2(total)
            for part in range(3):
                piece = level.astype(jnp.bfloat16).astype(jnp.float32)
                pieces[part].append(piece)
                level = level - piece
    if not turned:
        stats = jnp.concatenate(
            pieces[0] + pieces[1] + pieces[2] + [jnp.zeros((1, rows), jnp.float32)], axis=0
        ).astype(jnp.bfloat16)
        out_ref[feat : feat + 16, :] = stats[:, :half]
        rest[0][feat : feat + 16, :] = stats[:, half:]


def merge_call(a, b, turned):
    feat = a.shape[0] - 16
    rows = a.shape[1]
    if turned:
        out_shape = jax.ShapeDtypeStruct((rows, feat), jnp.bfloat16)
        out_specs = pl.BlockSpec(memory_space=pltpu.VMEM)
    else:
        out_shape = [jax.ShapeDtypeStruct((feat + 16, rows // 2), jnp.bfloat16)] * 2
        out_specs = [pl.BlockSpec(memory_space=pltpu.VMEM)] * 2
    return pl.pallas_call(
        functools.partial(merge_kernel, feat // DH, turned),
        in_specs=[pl.BlockSpec(memory_space=pltpu.VMEM)] * 2,
        out_specs=out_specs,
        out_shape=out_shape,
        compiler_params=pltpu.CompilerParams(vmem_limit_bytes=VMEM),
        cost_estimate=pl.CostEstimate(flops=0, bytes_accessed=6 << 20, transcendentals=0),
        name="merge",
    )(a, b)


def columns_kernel(ring, info, in_ref, *out_refs):
    width = out_refs[0].shape[1]
    core = jnp.bitwise_and(info[8], 1)
    for step, out_ref in enumerate(out_refs):
        target = jnp.bitwise_and(lax.shift_right_logical(info[9], 1) + step, ring - 1)
        half = core if step < ring else 1 - core
        begin = pl.multiple_of((2 * target + half) * width, DH)
        out_ref[...] = in_ref[:, pl.ds(begin, width)]


def column_blocks(weight, info, width, ring):
    rows, total = weight.shape
    return pl.pallas_call(
        functools.partial(columns_kernel, ring),
        grid=(rows // DH,),
        in_specs=[
            pl.BlockSpec(memory_space=pltpu.SMEM),
            pl.BlockSpec((DH, total), lambda i: (i, 0)),
        ],
        out_specs=[pl.BlockSpec((DH, width), lambda i: (i, 0))] * (ring + 1),
        out_shape=[jax.ShapeDtypeStruct((rows, width), weight.dtype)] * (ring + 1),
        compiler_params=pltpu.CompilerParams(vmem_limit_bytes=VMEM),
        cost_estimate=pl.CostEstimate(
            flops=0, bytes_accessed=4 * (ring + 1) * rows * width, transcendentals=0
        ),
        name="columns",
    )(info, weight)


def offer_kernel(info, in_ref, *out_refs):
    for mask, out_ref in enumerate(out_refs):
        owner = info[jnp.bitwise_xor(jnp.bitwise_and(info[8], 3), mask)]
        out_ref[...] = in_ref[lax.shift_right_logical(owner, 2)]


def offer_pieces(pieces, info):
    return pl.pallas_call(
        offer_kernel,
        in_specs=[
            pl.BlockSpec(memory_space=pltpu.SMEM),
            pl.BlockSpec(memory_space=pltpu.VMEM),
        ],
        out_specs=[pl.BlockSpec(memory_space=pltpu.VMEM)] * 4,
        out_shape=[jax.ShapeDtypeStruct(pieces.shape[1:], pieces.dtype)] * 4,
        compiler_params=pltpu.CompilerParams(vmem_limit_bytes=VMEM),
        name="offer",
    )(info, pieces)


def choose_kernel(info, *refs):
    kind = jnp.bitwise_and(info[8], 3)
    source = jnp.bitwise_xor(jnp.bitwise_and(info[kind], 3), kind)
    out_ref = refs[-1]
    for mask, in_ref in enumerate(refs[:-1]):

        @pl.when(source == mask)
        def _(in_ref=in_ref):
            out_ref[...] = in_ref[...]


def choose_piece(offers, info):
    return pl.pallas_call(
        choose_kernel,
        in_specs=[pl.BlockSpec(memory_space=pltpu.SMEM)]
        + [pl.BlockSpec(memory_space=pltpu.VMEM)] * len(offers),
        out_specs=pl.BlockSpec(memory_space=pltpu.VMEM),
        out_shape=jax.ShapeDtypeStruct(offers[0].shape, offers[0].dtype),
        compiler_params=pltpu.CompilerParams(vmem_limit_bytes=VMEM),
        name="choose",
    )(info, *offers)


def shards(
    queries, key_rows, value_rows, frame_ids, ctx_keys, ctx_values, owners, ctx_lengths, out_weight
):
    rows, feat = queries.shape
    blk_count = lax.axis_size("blk")
    head_devices = lax.axis_size("heads")
    plane, pair = 4, 2
    depth, ring_y = blk_count // plane, head_devices // pair
    me = lax.axis_index("blk")
    head_me = lax.axis_index("heads")
    info = jnp.concatenate([owners, ctx_lengths, me[None], head_me[None]]).astype(jnp.int32)
    columns = [[c + plane * z for z in range(depth)] for c in range(plane)]

    def shift(item, distance):
        steps = [(i, (i + plane * distance) % blk_count) for i in range(blk_count)]
        return lax.ppermute(item, "blk", steps)

    def swap(item, mask):
        return lax.ppermute(item, "blk", [(i, i ^ mask) for i in range(blk_count)])

    def shift_y(item, step):
        steps = [(i, (i + pair * step) % head_devices) for i in range(head_devices)]
        return lax.ppermute(item, "heads", steps)

    marks = jnp.pad(frame_ids.astype(jnp.bfloat16)[None], ((0, 15), (0, 2 * feat - rows)))
    mid = rows // 2
    part = ctx_keys.shape[1] // depth
    both = jnp.concatenate([key_rows, value_rows], axis=1)
    own = jnp.concatenate([both[:mid], jnp.zeros((part, 2 * feat), both.dtype), both[mid:], marks])
    query_own = jnp.concatenate([queries.T, marks[:, :rows]], axis=0)
    slot = jnp.concatenate([ctx_keys[0], ctx_values[0]], axis=1).reshape(depth, part, 2 * feat)

    ahead, behind = shift(own, 1), shift(own, -1)
    query_x, query_core, query_both = swap(query_own, 2), swap(query_own, 1), swap(query_own, 3)
    pieces = lax.all_to_all(slot, "blk", 0, 0, axis_index_groups=columns)
    slabs = column_blocks(out_weight, info, feat, ring_y)
    pieces, query_x, query_core, query_both, *slabs = lax.optimization_barrier(
        (pieces, query_x, query_core, query_both, *slabs)
    )
    offers = list(offer_pieces(pieces, info))
    offers = offers[:1] + [swap(offers[mask], mask) for mask in range(1, plane)]
    piece = choose_piece(offers, info)

    def loaded(item):
        return lax.dynamic_update_slice(item, piece, (mid, 0))

    def halves(item):
        return [(item, 0, mid), (item, mid + part, mid)], item

    def carried(item):
        return item, mid, part

    slab_own, slab_core = slabs[0], slabs[ring_y]
    *first, query_x, query_core, query_both, slab_near, slab_far, slab_back = (
        lax.optimization_barrier(
            (loaded(ahead), loaded(behind), query_x, query_core, query_both, *slabs[1:ring_y])
        )
    )
    query_plane = jnp.concatenate([query_own, query_x, query_core, query_both], axis=1)
    ahead, behind = shift(first[0], 1), shift(first[1], -1)
    *state, token = attention_call(
        query_plane, [halves(item) for item in (own, *first)], None, None, False, info
    )
    slab_near = shift_y(slab_near, 1)
    slab_back = shift_y(slab_back, ring_y - 1)
    slab_far = shift_y(slab_far, 2)

    *second, token = lax.optimization_barrier((ahead, behind, token))
    ahead, behind = shift(second[0], 1), shift(second[1], -1)
    *state, token = attention_call(
        query_plane, [halves(item) for item in second], state, None, False, token
    )
    ahead, behind, slab_near, slab_back, slab_far, token = lax.optimization_barrier(
        (ahead, behind, slab_near, slab_back, slab_far, token)
    )

    far_ahead, far_behind = shift(ahead[: mid + part], 1), shift(behind[mid:], -1)
    opposite = shift(ahead[mid : mid + part], 2)
    *state, token = attention_call(
        query_plane, [halves(ahead), halves(behind)], state, None, False, token
    )
    far = [(far_ahead, 0, mid), (far_behind, part, mid)], far_behind
    ctx = [
        (far_ahead, mid, part),
        carried(ahead),
        carried(second[0]),
        (piece, 0, part),
        carried(second[1]),
        carried(behind),
        (far_behind, 0, part),
        (opposite, 0, part),
    ]
    keep, send = attention_call(query_plane, [far, (ctx, None)], state, info, True, token)
    received = swap(send, 1)
    own, other = merge_call(keep, received, False)
    own_slabs = [slab_own, slab_near, slab_far, slab_back]
    core_slabs = [slab_core] + [swap(item, 1) for item in own_slabs[1:]]
    received, *core_slabs = lax.optimization_barrier((swap(other, 2), *core_slabs))
    attended = merge_call(own, received, True)

    def dots(block, step):
        return [
            jnp.dot(block, item[step], preferred_element_type=jnp.float32)
            for item in (own_slabs, core_slabs)
        ]

    total = dots(attended, 0)
    blocks = [(shift_y(attended, step), step) for step in (1, ring_y - 1, 2)]
    for block, step in blocks:
        block, *total = lax.optimization_barrier((block, *total))
        total = [old + new for old, new in zip(total, dots(block, step))]
    same = jnp.bitwise_and(jnp.bitwise_xor(me, head_me), 1) == 0
    mine = jnp.where(same, total[0], total[1])
    other = jnp.where(same, total[1], total[0])
    received = lax.ppermute(
        other.astype(jnp.bfloat16), "heads", [(i, i ^ 1) for i in range(head_devices)]
    )
    return (mine + received.astype(jnp.float32)).astype(jnp.bfloat16)


def solution(mesh):
    return jax.shard_map(
        shards,
        mesh=mesh,
        in_specs=(
            P("blk", "heads"),
            P("blk", "heads"),
            P("blk", "heads"),
            P("blk"),
            P("blk", None, "heads"),
            P("blk", None, "heads"),
            P(),
            P(),
            P("heads", None),
        ),
        out_specs=P("blk", "heads"),
        check_vma=False,
    )
```

```python
import functools
import math

import jax
import jax.numpy as jnp
from jax import lax
from jax.experimental import pallas as pl
from jax.experimental.pallas import tpu as pltpu
from jax.sharding import PartitionSpec as P

DH = 128
LOW = -1e30
MASKED = -3e30
FRAMES = 8
VMEM = 60 << 20


def scaled_exponent():
    return DH ** (-0.5) * math.log2(math.e)


def attention_kernel(layout, first, last, with_ctx, head_count, rows, *refs):
    refs = list(refs)
    ctx_info = refs.pop(0) if with_ctx else None
    refs.pop(0)
    query_ref = refs.pop(0)
    query_marks = refs.pop(0)
    chunks = []
    for segments, marked in layout:
        keys = [(refs.pop(0), refs.pop(0), begin, count) for begin, count in segments]
        chunks.append((keys, refs.pop(0) if marked else None))
    chunk_count = len(chunks)
    if not first:
        acc_in = refs.pop(0)
        stat_in = refs.pop(0)
    if last:
        keep_out = refs.pop(0)
        send_out = refs.pop(0)
    else:
        acc_out = refs.pop(0)
        stat_out = refs.pop(0)
        token_out = refs.pop(0)
    limits = refs.pop(0)
    bounds = refs.pop(0)
    if last:
        stats = refs.pop(0)
        levels = refs.pop(0)

    head = pl.program_id(0)
    span = query_ref.shape[1]
    lane = 128
    factor = scaled_exponent()

    @pl.when(head == 0)
    def _():
        for index, (_, mark_ref) in enumerate(chunks):
            if mark_ref is None:
                live = ctx_info[4 + jnp.bitwise_and(ctx_info[8], 3)]
                limits[index, 0:1, :] = jnp.full(
                    (1, span), live.astype(jnp.float32), jnp.float32
                )
                bounds[index] = jnp.int32(1)
                continue
            frame = lax.broadcasted_iota(jnp.int32, (FRAMES, rows), 0).astype(jnp.float32)
            key_marks = mark_ref[0:1, 0:rows].astype(jnp.float32)
            below = jnp.sum((key_marks <= frame).astype(jnp.float32), axis=1, keepdims=True)
            frame = lax.broadcasted_iota(jnp.int32, (FRAMES, span), 0).astype(jnp.float32)
            marks = query_marks[0:1, :].astype(jnp.float32)
            most = jnp.sum(jnp.where(marks == frame, below, 0.0), axis=0, keepdims=True)
            limits[index, 0:1, :] = most
            bounds[index] = jnp.max(most).astype(jnp.int32)

    def update():
        row = lax.broadcasted_iota(jnp.int32, (rows, lane), 0)
        places = [row.astype(jnp.float32)] * chunk_count
        if with_ctx:
            start = (lax.shift_right_logical(ctx_info[8], 2) + 5) * (rows // 8)
            places[-1] = jnp.bitwise_and(row + start, rows - 1).astype(jnp.float32)
        keys = [
            jnp.concatenate([ref[begin : begin + count] for ref, _, begin, count in segments])
            for segments, _ in chunks
        ]
        turned = [
            jnp.concatenate([ref[begin : begin + count] for _, ref, begin, count in segments]).T
            for segments, _ in chunks
        ]
        for tile in range(span // lane):
            spot = slice(tile * lane, (tile + 1) * lane)
            query = query_ref[:, spot]
            if first:
                top = jnp.full((1, lane), LOW, jnp.float32)
                total = jnp.zeros((1, lane), jnp.float32)
                acc = jnp.zeros((DH, lane), jnp.float32)
            else:
                top, total, acc = stat_in[0:1, spot], stat_in[1:2, spot], acc_in[:, spot]
            for index in range(chunk_count):
                scores = jnp.dot(keys[index], query, preferred_element_type=jnp.float32)
                scores = jnp.where(places[index] < limits[index, 0:1, spot], scores, MASKED)
                top_new = jnp.maximum(top, jnp.max(scores, axis=0, keepdims=True))
                weights = jnp.exp2((scores - top_new) * factor)
                fade = jnp.exp2((top - top_new) * factor)
                total = total * fade + jnp.sum(weights, axis=0, keepdims=True)
                acc = acc * fade + jnp.dot(
                    turned[index],
                    weights.astype(jnp.bfloat16),
                    preferred_element_type=jnp.float32,
                )
                top = top_new
            if not last:
                stat_out[0:1, spot] = top
                stat_out[1:2, spot] = total
                acc_out[:, spot] = acc
                continue
            out_ref, begin = (keep_out, 0) if tile * lane < rows else (send_out, rows)
            out_spot = slice(tile * lane - begin, (tile + 1) * lane - begin)
            out_ref[pl.ds(pl.multiple_of(head * DH, DH), DH), out_spot] = (
                acc * (1.0 / total)
            ).astype(jnp.bfloat16)
            levels[0:1, spot] = top * factor + jnp.log2(total)
        if last:
            level = levels[0:1, :]
            for part in range(3):
                piece = level.astype(jnp.bfloat16).astype(jnp.float32)
                stats[pl.ds(part * head_count + head, 1), :] = piece
                level = level - piece

    if first or last:
        update()
    else:
        seen = functools.reduce(jnp.maximum, [bounds[index] for index in range(chunk_count)]) > 0

        @pl.when(seen)
        def _():
            update()

        @pl.when(jnp.logical_not(seen))
        def _():
            acc_out[...] = acc_in[...]
            stat_out[0:2, :] = stat_in[0:2, :]

    if not last:
        token_out[...] = jnp.zeros_like(token_out)
    else:

        @pl.when(head == head_count - 1)
        def _():
            feat = head_count * DH
            keep_out[feat : feat + 16, :] = stats[:, :rows].astype(jnp.bfloat16)
            send_out[feat : feat + 16, :] = stats[:, rows:].astype(jnp.bfloat16)


def attention_call(queries, chunks, state, ctx_info, last, token, side=0):
    feat = queries.shape[0] - 16
    rows = queries.shape[1] // 4
    head_count = feat // DH
    first = state is None
    span = (2 if last else 4) * rows
    with_ctx = ctx_info is not None
    operands, specs = [], []
    if with_ctx:
        operands.append(ctx_info)
        specs.append(pl.BlockSpec(memory_space=pltpu.SMEM))
    operands += [token, queries, queries]
    specs.append(pl.BlockSpec(memory_space=pl.ANY))
    specs.append(pl.BlockSpec((DH, span), lambda h: (h, side)))
    specs.append(pl.BlockSpec((16, span), lambda h: (feat // 16, side)))
    layout = []
    for segments, marks in chunks:
        places = []
        for array, begin, count in segments:
            block, wanted = 0, count
            if begin % count == 0:
                block, begin = begin // count, 0
            else:
                count = array.shape[0]
            operands += [array, array]
            specs.append(pl.BlockSpec((count, DH), lambda h, at=block: (at, h)))
            specs.append(pl.BlockSpec((count, DH), lambda h, at=block: (at, head_count + h)))
            places.append((begin, wanted))
        layout.append((tuple(places), marks is not None))
        if marks is not None:
            operands.append(marks)
            specs.append(
                pl.BlockSpec((16, rows), lambda h, at=marks.shape[0] // 16 - 1: (at, 0))
            )
    aliases = {}
    state_specs = [
        pl.BlockSpec((DH, span), lambda h: (h, side)),
        pl.BlockSpec((8, span), lambda h: (h, side)),
    ]
    if not first:
        if not last:
            aliases = {len(operands): 0, len(operands) + 1: 1}
        operands.extend(state)
        specs.extend(state_specs)
    if last:
        out_shape = [jax.ShapeDtypeStruct((feat + 16, rows), jnp.bfloat16)] * 2
        out_specs = [pl.BlockSpec((feat + 16, rows), lambda h: (0, 0))] * 2
    else:
        out_shape = [
            jax.ShapeDtypeStruct((feat, span), jnp.float32),
            jax.ShapeDtypeStruct((8 * head_count, span), jnp.float32),
            jax.ShapeDtypeStruct((8, 128), jnp.float32),
        ]
        out_specs = state_specs + [pl.BlockSpec((8, 128), lambda h: (0, 0))]
    scratch = [
        pltpu.VMEM((len(chunks), 8, span), jnp.float32),
        pltpu.SMEM((len(chunks),), jnp.int32),
    ]
    if last:
        scratch += [
            pltpu.VMEM((16, span), jnp.float32),
            pltpu.VMEM((8, span), jnp.float32),
        ]
    return pl.pallas_call(
        functools.partial(
            attention_kernel, layout, first, last, with_ctx, head_count, rows
        ),
        grid=(head_count,),
        in_specs=specs,
        out_specs=out_specs,
        out_shape=out_shape,
        scratch_shapes=scratch,
        input_output_aliases=aliases,
        cost_estimate=pl.CostEstimate(
            flops=len(chunks) * span * 6 * 10**6, bytes_accessed=8 << 20, transcendentals=0
        ),
        compiler_params=pltpu.CompilerParams(vmem_limit_bytes=VMEM),
        name="attend",
    )(*operands)


def merge_kernel(head_count, turned, *refs):
    *in_refs, out_ref = refs
    feat = head_count * DH
    rows = in_refs[0].shape[1]
    stats = [ref[feat : feat + 16, :].astype(jnp.float32) for ref in in_refs]
    pieces = [[], [], []]
    for head in range(head_count):
        levels = [
            s[head : head + 1]
            + s[head_count + head : head_count + head + 1]
            + s[2 * head_count + head : 2 * head_count + head + 1]
            for s in stats
        ]
        top = functools.reduce(jnp.maximum, levels)
        shares = [jnp.exp2(level - top) for level in levels]
        total = sum(shares)
        inverse = 1.0 / total
        span = slice(head * DH, (head + 1) * DH)
        mixed = sum(
            ref[span, :].astype(jnp.float32) * (share * inverse)
            for ref, share in zip(in_refs, shares)
        )
        if turned:
            out_ref[:, span] = mixed.T.astype(jnp.bfloat16)
        else:
            out_ref[span, :] = mixed.astype(jnp.bfloat16)
            level = top + jnp.log2(total)
            for part in range(3):
                piece = level.astype(jnp.bfloat16).astype(jnp.float32)
                pieces[part].append(piece)
                level = level - piece
    if not turned:
        out_ref[feat : feat + 16, :] = jnp.concatenate(
            pieces[0] + pieces[1] + pieces[2] + [jnp.zeros((1, rows), jnp.float32)], axis=0
        ).astype(jnp.bfloat16)


def merge_call(parts, turned):
    feat = parts[0].shape[0] - 16
    rows = parts[0].shape[1]
    shape = (rows, feat) if turned else (feat + 16, rows)
    return pl.pallas_call(
        functools.partial(merge_kernel, feat // DH, turned),
        in_specs=[pl.BlockSpec(memory_space=pltpu.VMEM)] * len(parts),
        out_specs=pl.BlockSpec(memory_space=pltpu.VMEM),
        out_shape=jax.ShapeDtypeStruct(shape, jnp.bfloat16),
        compiler_params=pltpu.CompilerParams(vmem_limit_bytes=VMEM),
        cost_estimate=pl.CostEstimate(flops=0, bytes_accessed=1 << 10, transcendentals=0),
        name="merge",
    )(*parts)


def columns_kernel(ring, info, in_ref, *out_refs):
    width = out_refs[0].shape[1]
    core = jnp.bitwise_and(info[8], 1)
    for step, out_ref in enumerate(out_refs):
        target = jnp.bitwise_and(lax.shift_right_logical(info[9], 1) + step, ring - 1)
        half = core if step < ring else 1 - core
        begin = pl.multiple_of((2 * target + half) * width, DH)
        out_ref[...] = in_ref[:, pl.ds(begin, width)]


def column_blocks(weight, info, width, ring):
    rows, total = weight.shape
    return pl.pallas_call(
        functools.partial(columns_kernel, ring),
        grid=(rows // DH,),
        in_specs=[
            pl.BlockSpec(memory_space=pltpu.SMEM),
            pl.BlockSpec((DH, total), lambda i: (i, 0)),
        ],
        out_specs=[pl.BlockSpec((DH, width), lambda i: (i, 0))] * (ring + 1),
        out_shape=[jax.ShapeDtypeStruct((rows, width), weight.dtype)] * (ring + 1),
        compiler_params=pltpu.CompilerParams(vmem_limit_bytes=VMEM),
        cost_estimate=pl.CostEstimate(
            flops=0, bytes_accessed=4 * (ring + 1) * rows * width, transcendentals=0
        ),
        name="columns",
    )(info, weight)


def offer_kernel(info, in_ref, *out_refs):
    for mask, out_ref in enumerate(out_refs):
        owner = info[jnp.bitwise_xor(jnp.bitwise_and(info[8], 3), mask)]
        out_ref[...] = in_ref[lax.shift_right_logical(owner, 2)]


def offer_pieces(pieces, info):
    return pl.pallas_call(
        offer_kernel,
        in_specs=[
            pl.BlockSpec(memory_space=pltpu.SMEM),
            pl.BlockSpec(memory_space=pltpu.VMEM),
        ],
        out_specs=[pl.BlockSpec(memory_space=pltpu.VMEM)] * 4,
        out_shape=[jax.ShapeDtypeStruct(pieces.shape[1:], pieces.dtype)] * 4,
        compiler_params=pltpu.CompilerParams(vmem_limit_bytes=VMEM),
        name="offer",
    )(info, pieces)


def choose_kernel(info, *refs):
    kind = jnp.bitwise_and(info[8], 3)
    source = jnp.bitwise_xor(jnp.bitwise_and(info[kind], 3), kind)
    out_ref = refs[-1]
    for mask, in_ref in enumerate(refs[:-1]):

        @pl.when(source == mask)
        def _(in_ref=in_ref):
            out_ref[...] = in_ref[...]


def choose_piece(offers, info):
    return pl.pallas_call(
        choose_kernel,
        in_specs=[pl.BlockSpec(memory_space=pltpu.SMEM)]
        + [pl.BlockSpec(memory_space=pltpu.VMEM)] * len(offers),
        out_specs=pl.BlockSpec(memory_space=pltpu.VMEM),
        out_shape=jax.ShapeDtypeStruct(offers[0].shape, offers[0].dtype),
        compiler_params=pltpu.CompilerParams(vmem_limit_bytes=VMEM),
        name="choose",
    )(info, *offers)


def shards(
    queries, key_rows, value_rows, frame_ids, ctx_keys, ctx_values, owners, ctx_lengths, out_weight
):
    rows, feat = queries.shape
    blk_count = lax.axis_size("blk")
    head_devices = lax.axis_size("heads")
    plane, pair = 4, 2
    depth, ring_y = blk_count // plane, head_devices // pair
    me = lax.axis_index("blk")
    head_me = lax.axis_index("heads")
    info = jnp.concatenate([owners, ctx_lengths, me[None], head_me[None]]).astype(jnp.int32)
    columns = [[c + plane * z for z in range(depth)] for c in range(plane)]

    def shift(item, distance):
        steps = [(i, (i + plane * distance) % blk_count) for i in range(blk_count)]
        return lax.ppermute(item, "blk", steps)

    def swap(item, mask):
        return lax.ppermute(item, "blk", [(i, i ^ mask) for i in range(blk_count)])

    def shift_y(item, step):
        steps = [(i, (i + pair * step) % head_devices) for i in range(head_devices)]
        return lax.ppermute(item, "heads", steps)

    marks = jnp.pad(frame_ids.astype(jnp.bfloat16)[None], ((0, 15), (0, 2 * feat - rows)))
    mid = rows // 2
    part = ctx_keys.shape[1] // depth
    both = jnp.concatenate([key_rows, value_rows], axis=1)
    own = jnp.concatenate([both[:mid], jnp.zeros((part, 2 * feat), both.dtype), both[mid:], marks])
    query_own = jnp.concatenate([queries.T, marks[:, :rows]], axis=0)
    slot = jnp.concatenate([ctx_keys[0], ctx_values[0]], axis=1).reshape(depth, part, 2 * feat)

    ahead, behind = shift(own, 1), shift(own, -1)
    query_x, query_core = swap(query_own, 2), swap(query_own, 1)
    pieces = lax.all_to_all(slot, "blk", 0, 0, axis_index_groups=columns)
    slabs = column_blocks(out_weight, info, feat, ring_y)
    pieces, query_x, query_core, *slabs = lax.optimization_barrier(
        (pieces, query_x, query_core, *slabs)
    )
    offers = list(offer_pieces(pieces, info))
    offers = offers[:1] + [swap(offers[mask], mask) for mask in range(1, plane)]
    piece = choose_piece(offers, info)

    def loaded(item):
        return lax.dynamic_update_slice(item, piece, (mid, 0))

    def halves(item):
        return [(item, 0, mid), (item, mid + part, mid)], item

    def carried(item):
        return item, mid, part

    slab_own, slab_core = slabs[0], slabs[ring_y]
    *first, query_x, query_core, slab_near, slab_far, slab_back = lax.optimization_barrier(
        (loaded(ahead), loaded(behind), query_x, query_core, *slabs[1:ring_y])
    )
    query_both = swap(query_x, 1)
    query_plane = jnp.concatenate([query_x, query_both, query_own, query_core], axis=1)
    ahead, behind = shift(first[0], 1), shift(first[1], -1)
    *state, token = attention_call(
        query_plane, [halves(item) for item in (own, *first)], None, None, False, info
    )
    slab_near = shift_y(slab_near, 1)
    slab_back = shift_y(slab_back, ring_y - 1)
    slab_far = shift_y(slab_far, 2)

    *second, token = lax.optimization_barrier((ahead, behind, token))
    ahead, behind = shift(second[0], 1), shift(second[1], -1)
    *state, token = attention_call(
        query_plane, [halves(item) for item in second], state, None, False, token
    )
    ahead, behind, slab_near, slab_back, slab_far, token = lax.optimization_barrier(
        (ahead, behind, slab_near, slab_back, slab_far, token)
    )

    far_ahead, far_behind = shift(ahead[: mid + part], 1), shift(behind[mid:], -1)
    opposite = shift(ahead[mid : mid + part], 2)
    *state, token = attention_call(
        query_plane, [halves(ahead), halves(behind)], state, None, False, token
    )
    far = [(far_ahead, 0, mid), (far_behind, part, mid)], far_behind
    ctx = [
        (far_ahead, mid, part),
        carried(ahead),
        carried(second[0]),
        (piece, 0, part),
        carried(second[1]),
        carried(behind),
        (far_behind, 0, part),
        (opposite, 0, part),
    ]
    finish = [far, (ctx, None)]
    keep, send = attention_call(query_plane, finish, state, info, True, token, 0)
    other = merge_call([keep, swap(send, 1)], False)
    other, token = lax.optimization_barrier((other, token))
    keep, send = attention_call(query_plane, finish, state, info, True, token, 1)
    own_slabs = [slab_own, slab_near, slab_far, slab_back]
    core_slabs = [slab_core] + [swap(item, 1) for item in own_slabs[1:]]
    received, *core_slabs = lax.optimization_barrier((swap(other, 2), *core_slabs))
    own = merge_call([keep, received], False)
    attended = merge_call([own, swap(send, 1)], True)

    def dots(block, step):
        return [
            jnp.dot(block, item[step], preferred_element_type=jnp.float32)
            for item in (own_slabs, core_slabs)
        ]

    total = dots(attended, 0)
    blocks = [(shift_y(attended, step), step) for step in (1, ring_y - 1, 2)]
    for block, step in blocks:
        block, *total = lax.optimization_barrier((block, *total))
        total = [old + new for old, new in zip(total, dots(block, step))]
    same = jnp.bitwise_and(jnp.bitwise_xor(me, head_me), 1) == 0
    mine = jnp.where(same, total[0], total[1])
    other = jnp.where(same, total[1], total[0])
    received = lax.ppermute(
        other.astype(jnp.bfloat16), "heads", [(i, i ^ 1) for i in range(head_devices)]
    )
    return (mine + received.astype(jnp.float32)).astype(jnp.bfloat16)


def solution(mesh):
    return jax.shard_map(
        shards,
        mesh=mesh,
        in_specs=(
            P("blk", "heads"),
            P("blk", "heads"),
            P("blk", "heads"),
            P("blk"),
            P("blk", None, "heads"),
            P("blk", None, "heads"),
            P(),
            P(),
            P("heads", None),
        ),
        out_specs=P("blk", "heads"),
        check_vma=False,
    )
```

```python
import functools
import math

import jax
import jax.numpy as jnp
from jax import lax
from jax.experimental import pallas as pl
from jax.experimental.pallas import tpu as pltpu
from jax.sharding import PartitionSpec as P

DH = 128
LOW = -1e30
MASKED = -3e30
FRAMES = 8
VMEM = 60 << 20


def scaled_exponent():
    return DH ** (-0.5) * math.log2(math.e)


def attention_kernel(array_count, layout, first, last, with_ctx, head_count, rows, *refs):
    refs = list(refs)
    ctx_info = refs.pop(0) if with_ctx else None
    refs.pop(0)
    query_ref = refs.pop(0)
    query_marks = refs.pop(0)
    arrays = [refs.pop(0) for _ in range(array_count)]
    chunk_count = len(layout)
    if not first:
        acc_in = refs.pop(0)
        stat_in = refs.pop(0)
    if last:
        keep_out = refs.pop(0)
        send_out = refs.pop(0)
    else:
        acc_out = refs.pop(0)
        stat_out = refs.pop(0)
        token_out = refs.pop(0)
    limits = refs.pop(0)
    bounds = refs.pop(0)
    if last:
        stats = refs.pop(0)

    step = pl.program_id(0)
    heads = range(head_count) if last else [step]
    span = query_ref.shape[1]
    lane = 128
    factor = scaled_exponent()

    @pl.when(step == 0)
    def _():
        for index, (_, mark) in enumerate(layout):
            if mark is None:
                live = ctx_info[4 + jnp.bitwise_and(ctx_info[8], 3)]
                limits[index, 0:1, :] = jnp.full(
                    (1, span), live.astype(jnp.float32), jnp.float32
                )
                bounds[index] = jnp.int32(1)
                continue
            frame = lax.broadcasted_iota(jnp.int32, (FRAMES, rows), 0).astype(jnp.float32)
            marks_at, mark_row = mark
            key_marks = arrays[marks_at][mark_row : mark_row + 16, 0:rows][0:1].astype(jnp.float32)
            below = jnp.sum((key_marks <= frame).astype(jnp.float32), axis=1, keepdims=True)
            frame = lax.broadcasted_iota(jnp.int32, (FRAMES, span), 0).astype(jnp.float32)
            marks = query_marks[0:1, :].astype(jnp.float32)
            most = jnp.sum(jnp.where(marks == frame, below, 0.0), axis=0, keepdims=True)
            limits[index, 0:1, :] = most
            bounds[index] = jnp.max(most).astype(jnp.int32)

    def update(head, at):
        query_rows, stat_rows = slice(at * DH, (at + 1) * DH), at * 8
        row = lax.broadcasted_iota(jnp.int32, (rows, lane), 0)
        places = [row.astype(jnp.float32)] * chunk_count
        if with_ctx:
            start = (lax.shift_right_logical(ctx_info[8], 2) + 5) * (rows // 8)
            places[-1] = jnp.bitwise_and(row + start, rows - 1).astype(jnp.float32)

        def joined(segments, column):
            begin_lane = (column + head) * DH
            if not last:
                begin_lane = pl.multiple_of(begin_lane, DH)
            lanes = pl.ds(begin_lane, DH)
            return jnp.concatenate(
                [arrays[which][begin : begin + count, lanes] for which, begin, count in segments]
            )

        keys = [joined(segments, 0) for segments, _ in layout]
        turned = [joined(segments, head_count).T for segments, _ in layout]
        for tile in range(span // lane):
            spot = slice(tile * lane, (tile + 1) * lane)
            query = query_ref[query_rows, spot]
            if first:
                top = jnp.full((1, lane), LOW, jnp.float32)
                total = jnp.zeros((1, lane), jnp.float32)
                acc = jnp.zeros((DH, lane), jnp.float32)
            else:
                top = stat_in[stat_rows : stat_rows + 1, spot]
                total = stat_in[stat_rows + 1 : stat_rows + 2, spot]
                acc = acc_in[query_rows, spot]
            for index in range(chunk_count):
                scores = jnp.dot(keys[index], query, preferred_element_type=jnp.float32)
                scores = jnp.where(places[index] < limits[index, 0:1, spot], scores, MASKED)
                top_new = jnp.maximum(top, jnp.max(scores, axis=0, keepdims=True))
                weights = jnp.exp2((scores - top_new) * factor)
                fade = jnp.exp2((top - top_new) * factor)
                total = total * fade + jnp.sum(weights, axis=0, keepdims=True)
                acc = acc * fade + jnp.dot(
                    turned[index],
                    weights.astype(jnp.bfloat16),
                    preferred_element_type=jnp.float32,
                )
                top = top_new
            if not last:
                stat_out[0:1, spot] = top
                stat_out[1:2, spot] = total
                acc_out[:, spot] = acc
                continue
            out_ref, begin = (keep_out, 0) if tile * lane < rows else (send_out, rows)
            out_spot = slice(tile * lane - begin, (tile + 1) * lane - begin)
            out_ref[query_rows, out_spot] = (acc * (1.0 / total)).astype(jnp.bfloat16)
            level = top * factor + jnp.log2(total)
            for part in range(3):
                piece = level.astype(jnp.bfloat16).astype(jnp.float32)
                stats[part * head_count + head : part * head_count + head + 1, spot] = piece
                level = level - piece

    if first or last:
        for at, head in enumerate(heads):
            update(head, at)
    else:
        seen = functools.reduce(jnp.maximum, [bounds[index] for index in range(chunk_count)]) > 0

        @pl.when(seen)
        def _():
            update(step, 0)

        @pl.when(jnp.logical_not(seen))
        def _():
            acc_out[...] = acc_in[...]
            stat_out[0:2, :] = stat_in[0:2, :]

    if not last:
        token_out[...] = jnp.zeros_like(token_out)
    else:
        feat = head_count * DH
        keep_out[feat : feat + 16, :] = stats[:, :rows].astype(jnp.bfloat16)
        send_out[feat : feat + 16, :] = stats[:, rows:].astype(jnp.bfloat16)


def attention_call(queries, chunks, state, ctx_info, last, token, side=0):
    feat = queries.shape[0] - 16
    rows = queries.shape[1] // 4
    head_count = feat // DH
    first = state is None
    span = (2 if last else 4) * rows
    steps = 1 if last else head_count
    high = head_count // steps
    with_ctx = ctx_info is not None
    operands, specs = [], []
    if with_ctx:
        operands.append(ctx_info)
        specs.append(pl.BlockSpec(memory_space=pltpu.SMEM))
    operands += [token, queries, queries]
    specs.append(pl.BlockSpec(memory_space=pl.ANY))
    specs.append(pl.BlockSpec((high * DH, span), lambda h: (h, side)))
    specs.append(pl.BlockSpec((16, span), lambda h: (feat // 16, side)))
    found = []
    for segments, _ in chunks:
        for array, begin, count in segments:
            for known, places in found:
                if known is array:
                    places.add((begin, count))
                    break
            else:
                found.append((array, {(begin, count)}))
    starts = []
    for array, places in found:
        begin, count = min(places)
        exact = len(places) == 1 and begin % count == 0
        operands.append(array)
        shape = (count if exact else array.shape[0], array.shape[1])
        at = begin // count if exact else 0
        specs.append(pl.BlockSpec(shape, lambda h, at=at: (at, 0)))
        starts.append(begin if exact else 0)

    def number(array):
        return next(at for at, (known, _) in enumerate(found) if known is array)

    layout = []
    for segments, marks in chunks:
        parts = tuple(
            (number(array), begin - starts[number(array)], count)
            for array, begin, count in segments
        )
        layout.append((parts, None if marks is None else (number(marks), marks.shape[0] - 16)))
    aliases = {}
    state_specs = [
        pl.BlockSpec((high * DH, span), lambda h: (h, side)),
        pl.BlockSpec((high * 8, span), lambda h: (h, side)),
    ]
    if not first:
        if not last:
            aliases = {len(operands): 0, len(operands) + 1: 1}
        operands.extend(state)
        specs.extend(state_specs)
    if last:
        out_shape = [jax.ShapeDtypeStruct((feat + 16, rows), jnp.bfloat16)] * 2
        out_specs = [pl.BlockSpec((feat + 16, rows), lambda h: (0, 0))] * 2
    else:
        out_shape = [
            jax.ShapeDtypeStruct((feat, span), jnp.float32),
            jax.ShapeDtypeStruct((8 * head_count, span), jnp.float32),
            jax.ShapeDtypeStruct((8, 128), jnp.float32),
        ]
        out_specs = state_specs + [pl.BlockSpec((8, 128), lambda h: (0, 0))]
    scratch = [
        pltpu.VMEM((len(chunks), 8, span), jnp.float32),
        pltpu.SMEM((len(chunks),), jnp.int32),
    ]
    if last:
        scratch.append(pltpu.VMEM((16, span), jnp.float32))
    return pl.pallas_call(
        functools.partial(
            attention_kernel, len(found), layout, first, last, with_ctx, head_count, rows
        ),
        grid=(steps,),
        in_specs=specs,
        out_specs=out_specs,
        out_shape=out_shape,
        scratch_shapes=scratch,
        input_output_aliases=aliases,
        cost_estimate=pl.CostEstimate(
            flops=len(chunks) * span * 6 * 10**6, bytes_accessed=8 << 20, transcendentals=0
        ),
        compiler_params=pltpu.CompilerParams(vmem_limit_bytes=VMEM),
        name="attend",
    )(*operands)


def merge_kernel(head_count, turned, *refs):
    *in_refs, out_ref = refs
    feat = head_count * DH
    rows = in_refs[0].shape[1]
    stats = [ref[feat : feat + 16, :].astype(jnp.float32) for ref in in_refs]
    pieces = [[], [], []]
    for head in range(head_count):
        levels = [
            s[head : head + 1]
            + s[head_count + head : head_count + head + 1]
            + s[2 * head_count + head : 2 * head_count + head + 1]
            for s in stats
        ]
        top = functools.reduce(jnp.maximum, levels)
        shares = [jnp.exp2(level - top) for level in levels]
        total = sum(shares)
        inverse = 1.0 / total
        span = slice(head * DH, (head + 1) * DH)
        mixed = sum(
            ref[span, :].astype(jnp.float32) * (share * inverse)
            for ref, share in zip(in_refs, shares)
        )
        if turned:
            out_ref[:, span] = mixed.T.astype(jnp.bfloat16)
        else:
            out_ref[span, :] = mixed.astype(jnp.bfloat16)
            level = top + jnp.log2(total)
            for part in range(3):
                piece = level.astype(jnp.bfloat16).astype(jnp.float32)
                pieces[part].append(piece)
                level = level - piece
    if not turned:
        out_ref[feat : feat + 16, :] = jnp.concatenate(
            pieces[0] + pieces[1] + pieces[2] + [jnp.zeros((1, rows), jnp.float32)], axis=0
        ).astype(jnp.bfloat16)


def merge_call(parts, turned):
    feat = parts[0].shape[0] - 16
    rows = parts[0].shape[1]
    shape = (rows, feat) if turned else (feat + 16, rows)
    return pl.pallas_call(
        functools.partial(merge_kernel, feat // DH, turned),
        in_specs=[pl.BlockSpec(memory_space=pltpu.VMEM)] * len(parts),
        out_specs=pl.BlockSpec(memory_space=pltpu.VMEM),
        out_shape=jax.ShapeDtypeStruct(shape, jnp.bfloat16),
        compiler_params=pltpu.CompilerParams(vmem_limit_bytes=VMEM),
        cost_estimate=pl.CostEstimate(flops=0, bytes_accessed=1 << 10, transcendentals=0),
        name="merge",
    )(*parts)


def columns_kernel(ring, info, in_ref, *out_refs):
    width = out_refs[0].shape[1]
    core = jnp.bitwise_and(info[8], 1)
    for step, out_ref in enumerate(out_refs):
        target = jnp.bitwise_and(lax.shift_right_logical(info[9], 1) + step, ring - 1)
        half = core if step < ring else 1 - core
        begin = pl.multiple_of((2 * target + half) * width, DH)
        out_ref[...] = in_ref[:, pl.ds(begin, width)]


def column_blocks(weight, info, width, ring):
    rows, total = weight.shape
    return pl.pallas_call(
        functools.partial(columns_kernel, ring),
        grid=(rows // DH,),
        in_specs=[
            pl.BlockSpec(memory_space=pltpu.SMEM),
            pl.BlockSpec((DH, total), lambda i: (i, 0)),
        ],
        out_specs=[pl.BlockSpec((DH, width), lambda i: (i, 0))] * (ring + 1),
        out_shape=[jax.ShapeDtypeStruct((rows, width), weight.dtype)] * (ring + 1),
        compiler_params=pltpu.CompilerParams(vmem_limit_bytes=VMEM),
        cost_estimate=pl.CostEstimate(
            flops=0, bytes_accessed=4 * (ring + 1) * rows * width, transcendentals=0
        ),
        name="columns",
    )(info, weight)


def offer_kernel(info, in_ref, *out_refs):
    for mask, out_ref in enumerate(out_refs):
        owner = info[jnp.bitwise_xor(jnp.bitwise_and(info[8], 3), mask)]
        out_ref[...] = in_ref[lax.shift_right_logical(owner, 2)]


def offer_pieces(pieces, info):
    return pl.pallas_call(
        offer_kernel,
        in_specs=[
            pl.BlockSpec(memory_space=pltpu.SMEM),
            pl.BlockSpec(memory_space=pltpu.VMEM),
        ],
        out_specs=[pl.BlockSpec(memory_space=pltpu.VMEM)] * 4,
        out_shape=[jax.ShapeDtypeStruct(pieces.shape[1:], pieces.dtype)] * 4,
        compiler_params=pltpu.CompilerParams(vmem_limit_bytes=VMEM),
        name="offer",
    )(info, pieces)


def choose_kernel(info, *refs):
    kind = jnp.bitwise_and(info[8], 3)
    source = jnp.bitwise_xor(jnp.bitwise_and(info[kind], 3), kind)
    out_ref = refs[-1]
    for mask, in_ref in enumerate(refs[:-1]):

        @pl.when(source == mask)
        def _(in_ref=in_ref):
            out_ref[...] = in_ref[...]


def choose_piece(offers, info):
    return pl.pallas_call(
        choose_kernel,
        in_specs=[pl.BlockSpec(memory_space=pltpu.SMEM)]
        + [pl.BlockSpec(memory_space=pltpu.VMEM)] * len(offers),
        out_specs=pl.BlockSpec(memory_space=pltpu.VMEM),
        out_shape=jax.ShapeDtypeStruct(offers[0].shape, offers[0].dtype),
        compiler_params=pltpu.CompilerParams(vmem_limit_bytes=VMEM),
        name="choose",
    )(info, *offers)


def shards(
    queries, key_rows, value_rows, frame_ids, ctx_keys, ctx_values, owners, ctx_lengths, out_weight
):
    rows, feat = queries.shape
    blk_count = lax.axis_size("blk")
    head_devices = lax.axis_size("heads")
    plane, pair = 4, 2
    depth, ring_y = blk_count // plane, head_devices // pair
    me = lax.axis_index("blk")
    head_me = lax.axis_index("heads")
    info = jnp.concatenate([owners, ctx_lengths, me[None], head_me[None]]).astype(jnp.int32)
    columns = [[c + plane * z for z in range(depth)] for c in range(plane)]

    def shift(item, distance):
        steps = [(i, (i + plane * distance) % blk_count) for i in range(blk_count)]
        return lax.ppermute(item, "blk", steps)

    def swap(item, mask):
        return lax.ppermute(item, "blk", [(i, i ^ mask) for i in range(blk_count)])

    def shift_y(item, step):
        steps = [(i, (i + pair * step) % head_devices) for i in range(head_devices)]
        return lax.ppermute(item, "heads", steps)

    marks = jnp.pad(frame_ids.astype(jnp.bfloat16)[None], ((0, 15), (0, 2 * feat - rows)))
    mid = rows // 2
    part = ctx_keys.shape[1] // depth
    both = jnp.concatenate([key_rows, value_rows], axis=1)
    own = jnp.concatenate([both[:mid], jnp.zeros((part, 2 * feat), both.dtype), both[mid:], marks])
    query_own = jnp.concatenate([queries.T, marks[:, :rows]], axis=0)
    slot = jnp.concatenate([ctx_keys[0], ctx_values[0]], axis=1).reshape(depth, part, 2 * feat)

    ahead, behind = shift(own, 1), shift(own, -1)
    query_x, query_core = swap(query_own, 2), swap(query_own, 1)
    pieces = lax.all_to_all(slot, "blk", 0, 0, axis_index_groups=columns)
    slabs = column_blocks(out_weight, info, feat, ring_y)
    pieces, query_x, query_core, *slabs = lax.optimization_barrier(
        (pieces, query_x, query_core, *slabs)
    )
    offers = list(offer_pieces(pieces, info))
    offers = offers[:1] + [swap(offers[mask], mask) for mask in range(1, plane)]
    piece = choose_piece(offers, info)

    def loaded(item):
        return lax.dynamic_update_slice(item, piece, (mid, 0))

    def halves(item):
        return [(item, 0, mid), (item, mid + part, mid)], item

    def carried(item):
        return item, mid, part

    slab_own, slab_core = slabs[0], slabs[ring_y]
    *first, query_x, query_core, slab_near, slab_far, slab_back = lax.optimization_barrier(
        (loaded(ahead), loaded(behind), query_x, query_core, *slabs[1:ring_y])
    )
    query_both = swap(query_x, 1)
    query_plane = jnp.concatenate([query_x, query_both, query_own, query_core], axis=1)
    ahead, behind = shift(first[0], 1), shift(first[1], -1)
    *state, token = attention_call(
        query_plane, [halves(item) for item in (own, *first)], None, None, False, info
    )
    slab_near = shift_y(slab_near, 1)
    slab_back = shift_y(slab_back, ring_y - 1)
    slab_far = shift_y(slab_far, 2)

    *second, token = lax.optimization_barrier((ahead, behind, token))
    ahead, behind = shift(second[0], 1), shift(second[1], -1)
    *state, token = attention_call(
        query_plane, [halves(item) for item in second], state, None, False, token
    )
    ahead, behind, slab_near, slab_back, slab_far, token = lax.optimization_barrier(
        (ahead, behind, slab_near, slab_back, slab_far, token)
    )

    far_ahead, far_behind = shift(ahead[: mid + part], 1), shift(behind[mid:], -1)
    opposite = shift(ahead[mid : mid + part], 2)
    *state, token = attention_call(
        query_plane, [halves(ahead), halves(behind)], state, None, False, token
    )
    far = [(far_ahead, 0, mid), (far_behind, part, mid)], far_behind
    ctx = [
        (far_ahead, mid, part),
        carried(ahead),
        carried(second[0]),
        (piece, 0, part),
        carried(second[1]),
        carried(behind),
        (far_behind, 0, part),
        (opposite, 0, part),
    ]
    finish = [far, (ctx, None)]
    keep, send = attention_call(query_plane, finish, state, info, True, token, 0)
    other = merge_call([keep, swap(send, 1)], False)
    other, token = lax.optimization_barrier((other, token))
    keep, send = attention_call(query_plane, finish, state, info, True, token, 1)
    own_slabs = [slab_own, slab_near, slab_far, slab_back]
    core_slabs = [slab_core] + [swap(item, 1) for item in own_slabs[1:]]
    received, *core_slabs = lax.optimization_barrier((swap(other, 2), *core_slabs))
    own = merge_call([keep, received], False)
    attended = merge_call([own, swap(send, 1)], True)

    def dots(block, step):
        return [
            jnp.dot(block, item[step], preferred_element_type=jnp.float32)
            for item in (own_slabs, core_slabs)
        ]

    total = dots(attended, 0)
    blocks = [(shift_y(attended, step), step) for step in (1, ring_y - 1, 2)]
    for block, step in blocks:
        block, *total = lax.optimization_barrier((block, *total))
        total = [old + new for old, new in zip(total, dots(block, step))]
    same = jnp.bitwise_and(jnp.bitwise_xor(me, head_me), 1) == 0
    mine = jnp.where(same, total[0], total[1])
    other = jnp.where(same, total[1], total[0])
    received = lax.ppermute(
        other.astype(jnp.bfloat16), "heads", [(i, i ^ 1) for i in range(head_devices)]
    )
    return (mine + received.astype(jnp.float32)).astype(jnp.bfloat16)


def solution(mesh):
    return jax.shard_map(
        shards,
        mesh=mesh,
        in_specs=(
            P("blk", "heads"),
            P("blk", "heads"),
            P("blk", "heads"),
            P("blk"),
            P("blk", None, "heads"),
            P("blk", None, "heads"),
            P(),
            P(),
            P("heads", None),
        ),
        out_specs=P("blk", "heads"),
        check_vma=False,
    )
```

```python
import functools
import math

import jax
import jax.numpy as jnp
from jax import lax
from jax.experimental import pallas as pl
from jax.experimental.pallas import tpu as pltpu
from jax.sharding import PartitionSpec as P

DH = 128
LOW = -1e30
MASKED = -3e30
FRAMES = 8
VMEM = 60 << 20


def scaled_exponent():
    return DH ** (-0.5) * math.log2(math.e)


def attention_kernel(array_count, layout, first, last, with_ctx, head_count, rows, *refs):
    refs = list(refs)
    ctx_info = refs.pop(0) if with_ctx else None
    refs.pop(0)
    query_ref = refs.pop(0)
    query_marks = refs.pop(0)
    arrays = [refs.pop(0) for _ in range(array_count)]
    chunk_count = len(layout)
    if not first:
        acc_in = refs.pop(0)
        stat_in = refs.pop(0)
    if last:
        keep_out = refs.pop(0)
        send_out = refs.pop(0)
    else:
        acc_out = refs.pop(0)
        stat_out = refs.pop(0)
        token_out = refs.pop(0)
    limits = refs.pop(0)
    bounds = refs.pop(0)
    if last:
        stats = refs.pop(0)

    step = pl.program_id(0)
    heads = range(head_count) if last else [step]
    span = query_ref.shape[1]
    lane = 128
    factor = scaled_exponent()

    @pl.when(step == 0)
    def _():
        for index, (_, mark) in enumerate(layout):
            if mark is None:
                live = ctx_info[4 + jnp.bitwise_and(ctx_info[8], 3)]
                limits[index, 0:1, :] = jnp.full(
                    (1, span), live.astype(jnp.float32), jnp.float32
                )
                bounds[index] = jnp.int32(1)
                continue
            frame = lax.broadcasted_iota(jnp.int32, (FRAMES, rows), 0).astype(jnp.float32)
            marks_at, mark_row = mark
            key_marks = arrays[marks_at][mark_row : mark_row + 16, 0:rows][0:1].astype(jnp.float32)
            below = jnp.sum((key_marks <= frame).astype(jnp.float32), axis=1, keepdims=True)
            frame = lax.broadcasted_iota(jnp.int32, (FRAMES, span), 0).astype(jnp.float32)
            marks = query_marks[0:1, :].astype(jnp.float32)
            most = jnp.sum(jnp.where(marks == frame, below, 0.0), axis=0, keepdims=True)
            limits[index, 0:1, :] = most
            bounds[index] = jnp.max(most).astype(jnp.int32)

    def update(head, at):
        query_rows, stat_rows = slice(at * DH, (at + 1) * DH), at * 8
        row = lax.broadcasted_iota(jnp.int32, (rows, lane), 0)
        places = [row.astype(jnp.float32)] * chunk_count
        if with_ctx:
            start = (lax.shift_right_logical(ctx_info[8], 2) + 5) * (rows // 8)
            places[-1] = jnp.bitwise_and(row + start, rows - 1).astype(jnp.float32)

        def joined(segments, column):
            begin_lane = (column + head) * DH
            if not last:
                begin_lane = pl.multiple_of(begin_lane, DH)
            lanes = pl.ds(begin_lane, DH)
            return jnp.concatenate(
                [arrays[which][begin : begin + count, lanes] for which, begin, count in segments]
            )

        keys = [joined(segments, 0) for segments, _ in layout]
        turned = [joined(segments, head_count).T for segments, _ in layout]
        for tile in range(span // lane):
            spot = slice(tile * lane, (tile + 1) * lane)
            query = query_ref[query_rows, spot]
            if first:
                top = jnp.full((1, lane), LOW, jnp.float32)
                total = jnp.zeros((1, lane), jnp.float32)
                acc = jnp.zeros((DH, lane), jnp.float32)
            else:
                top = stat_in[stat_rows : stat_rows + 1, spot]
                total = stat_in[stat_rows + 1 : stat_rows + 2, spot]
                acc = acc_in[query_rows, spot]
            for index in range(chunk_count):
                scores = jnp.dot(keys[index], query, preferred_element_type=jnp.float32)
                scores = jnp.where(places[index] < limits[index, 0:1, spot], scores, MASKED)
                top_new = jnp.maximum(top, jnp.max(scores, axis=0, keepdims=True))
                weights = jnp.exp2((scores - top_new) * factor)
                fade = jnp.exp2((top - top_new) * factor)
                total = total * fade + jnp.sum(weights, axis=0, keepdims=True)
                acc = acc * fade + jnp.dot(
                    turned[index],
                    weights.astype(jnp.bfloat16),
                    preferred_element_type=jnp.float32,
                )
                top = top_new
            if not last:
                stat_out[0:1, spot] = top
                stat_out[1:2, spot] = total
                acc_out[:, spot] = acc
                continue
            out_ref, begin = (keep_out, 0) if tile * lane < rows else (send_out, rows)
            out_spot = slice(tile * lane - begin, (tile + 1) * lane - begin)
            out_ref[query_rows, out_spot] = (acc * (1.0 / total)).astype(jnp.bfloat16)
            level = top * factor + jnp.log2(total)
            for part in range(3):
                piece = level.astype(jnp.bfloat16).astype(jnp.float32)
                stats[part * head_count + head : part * head_count + head + 1, spot] = piece
                level = level - piece

    if first or last:
        for at, head in enumerate(heads):
            update(head, at)
    else:
        seen = functools.reduce(jnp.maximum, [bounds[index] for index in range(chunk_count)]) > 0

        @pl.when(seen)
        def _():
            update(step, 0)

        @pl.when(jnp.logical_not(seen))
        def _():
            acc_out[...] = acc_in[...]
            stat_out[0:2, :] = stat_in[0:2, :]

    if not last:
        token_out[...] = jnp.zeros_like(token_out)
    else:
        feat = head_count * DH
        keep_out[feat : feat + 16, :] = stats[:, :rows].astype(jnp.bfloat16)
        send_out[feat : feat + 16, :] = stats[:, rows:].astype(jnp.bfloat16)


def attention_call(queries, chunks, state, ctx_info, last, token, side=0):
    feat = queries.shape[0] - 16
    rows = queries.shape[1] // 4
    head_count = feat // DH
    first = state is None
    span = (2 if last else 4) * rows
    steps = 1 if last else head_count
    high = head_count // steps
    with_ctx = ctx_info is not None
    operands, specs = [], []
    if with_ctx:
        operands.append(ctx_info)
        specs.append(pl.BlockSpec(memory_space=pltpu.SMEM))
    operands += [token, queries, queries]
    specs.append(pl.BlockSpec(memory_space=pl.ANY))
    specs.append(pl.BlockSpec((high * DH, span), lambda h: (h, side)))
    specs.append(pl.BlockSpec((16, span), lambda h: (feat // 16, side)))
    found = []
    for segments, _ in chunks:
        for array, begin, count in segments:
            for known, places in found:
                if known is array:
                    places.add((begin, count))
                    break
            else:
                found.append((array, {(begin, count)}))
    starts = []
    for array, places in found:
        begin, count = min(places)
        exact = len(places) == 1 and begin % count == 0
        operands.append(array)
        shape = (count if exact else array.shape[0], array.shape[1])
        at = begin // count if exact else 0
        specs.append(pl.BlockSpec(shape, lambda h, at=at: (at, 0)))
        starts.append(begin if exact else 0)

    def number(array):
        return next(at for at, (known, _) in enumerate(found) if known is array)

    layout = []
    for segments, marks in chunks:
        parts = tuple(
            (number(array), begin - starts[number(array)], count)
            for array, begin, count in segments
        )
        layout.append((parts, None if marks is None else (number(marks), marks.shape[0] - 16)))
    aliases = {}
    state_specs = [
        pl.BlockSpec((high * DH, span), lambda h: (h, side)),
        pl.BlockSpec((high * 8, span), lambda h: (h, side)),
    ]
    if not first:
        if not last:
            aliases = {len(operands): 0, len(operands) + 1: 1}
        operands.extend(state)
        specs.extend(state_specs)
    if last:
        out_shape = [jax.ShapeDtypeStruct((feat + 16, rows), jnp.bfloat16)] * 2
        out_specs = [pl.BlockSpec((feat + 16, rows), lambda h: (0, 0))] * 2
    else:
        out_shape = [
            jax.ShapeDtypeStruct((feat, span), jnp.float32),
            jax.ShapeDtypeStruct((8 * head_count, span), jnp.float32),
            jax.ShapeDtypeStruct((8, 128), jnp.float32),
        ]
        out_specs = state_specs + [pl.BlockSpec((8, 128), lambda h: (0, 0))]
    scratch = [
        pltpu.VMEM((len(chunks), 8, span), jnp.float32),
        pltpu.SMEM((len(chunks),), jnp.int32),
    ]
    if last:
        scratch.append(pltpu.VMEM((16, span), jnp.float32))
    return pl.pallas_call(
        functools.partial(
            attention_kernel, len(found), layout, first, last, with_ctx, head_count, rows
        ),
        grid=(steps,),
        in_specs=specs,
        out_specs=out_specs,
        out_shape=out_shape,
        scratch_shapes=scratch,
        input_output_aliases=aliases,
        cost_estimate=pl.CostEstimate(
            flops=len(chunks) * span * 6 * 10**6, bytes_accessed=8 << 20, transcendentals=0
        ),
        compiler_params=pltpu.CompilerParams(vmem_limit_bytes=VMEM),
        name="attend",
    )(*operands)


def merge_kernel(head_count, turned, *refs):
    *in_refs, out_ref = refs
    feat = head_count * DH
    rows = in_refs[0].shape[1]
    stats = [ref[feat : feat + 16, :].astype(jnp.float32) for ref in in_refs]
    pieces = [[], [], []]
    for head in range(head_count):
        levels = [
            s[head : head + 1]
            + s[head_count + head : head_count + head + 1]
            + s[2 * head_count + head : 2 * head_count + head + 1]
            for s in stats
        ]
        top = functools.reduce(jnp.maximum, levels)
        shares = [jnp.exp2(level - top) for level in levels]
        total = sum(shares)
        inverse = 1.0 / total
        span = slice(head * DH, (head + 1) * DH)
        mixed = sum(
            ref[span, :].astype(jnp.float32) * (share * inverse)
            for ref, share in zip(in_refs, shares)
        )
        if turned:
            out_ref[:, span] = mixed.T.astype(jnp.bfloat16)
        else:
            out_ref[span, :] = mixed.astype(jnp.bfloat16)
            level = top + jnp.log2(total)
            for part in range(3):
                piece = level.astype(jnp.bfloat16).astype(jnp.float32)
                pieces[part].append(piece)
                level = level - piece
    if not turned:
        out_ref[feat : feat + 16, :] = jnp.concatenate(
            pieces[0] + pieces[1] + pieces[2] + [jnp.zeros((1, rows), jnp.float32)], axis=0
        ).astype(jnp.bfloat16)


def merge_call(parts, turned):
    feat = parts[0].shape[0] - 16
    rows = parts[0].shape[1]
    shape = (rows, feat) if turned else (feat + 16, rows)
    return pl.pallas_call(
        functools.partial(merge_kernel, feat // DH, turned),
        in_specs=[pl.BlockSpec(memory_space=pltpu.VMEM)] * len(parts),
        out_specs=pl.BlockSpec(memory_space=pltpu.VMEM),
        out_shape=jax.ShapeDtypeStruct(shape, jnp.bfloat16),
        compiler_params=pltpu.CompilerParams(vmem_limit_bytes=VMEM),
        cost_estimate=pl.CostEstimate(flops=0, bytes_accessed=1 << 10, transcendentals=0),
        name="merge",
    )(*parts)


def columns_kernel(ring, info, in_ref, *out_refs):
    width = out_refs[0].shape[1]
    core = jnp.bitwise_and(info[8], 1)
    for step, out_ref in enumerate(out_refs):
        target = jnp.bitwise_and(lax.shift_right_logical(info[9], 1) + step, ring - 1)
        half = core if step < ring else 1 - core
        begin = pl.multiple_of((2 * target + half) * width, DH)
        out_ref[...] = in_ref[:, pl.ds(begin, width)]


def column_blocks(weight, info, width, ring):
    rows, total = weight.shape
    return pl.pallas_call(
        functools.partial(columns_kernel, ring),
        grid=(rows // DH,),
        in_specs=[
            pl.BlockSpec(memory_space=pltpu.SMEM),
            pl.BlockSpec((DH, total), lambda i: (i, 0)),
        ],
        out_specs=[pl.BlockSpec((DH, width), lambda i: (i, 0))] * (ring + 1),
        out_shape=[jax.ShapeDtypeStruct((rows, width), weight.dtype)] * (ring + 1),
        compiler_params=pltpu.CompilerParams(vmem_limit_bytes=VMEM),
        cost_estimate=pl.CostEstimate(
            flops=0, bytes_accessed=4 * (ring + 1) * rows * width, transcendentals=0
        ),
        name="columns",
    )(info, weight)


def offer_kernel(info, in_ref, *out_refs):
    for mask, out_ref in enumerate(out_refs):
        owner = info[jnp.bitwise_xor(jnp.bitwise_and(info[8], 3), mask)]
        out_ref[...] = in_ref[lax.shift_right_logical(owner, 2)]


def offer_pieces(pieces, info):
    return pl.pallas_call(
        offer_kernel,
        in_specs=[
            pl.BlockSpec(memory_space=pltpu.SMEM),
            pl.BlockSpec(memory_space=pltpu.VMEM),
        ],
        out_specs=[pl.BlockSpec(memory_space=pltpu.VMEM)] * 4,
        out_shape=[jax.ShapeDtypeStruct(pieces.shape[1:], pieces.dtype)] * 4,
        compiler_params=pltpu.CompilerParams(vmem_limit_bytes=VMEM),
        name="offer",
    )(info, pieces)


def choose_kernel(info, *refs):
    kind = jnp.bitwise_and(info[8], 3)
    source = jnp.bitwise_xor(jnp.bitwise_and(info[kind], 3), kind)
    out_ref = refs[-1]
    for mask, in_ref in enumerate(refs[:-1]):

        @pl.when(source == mask)
        def _(in_ref=in_ref):
            out_ref[...] = in_ref[...]


def choose_piece(offers, info):
    return pl.pallas_call(
        choose_kernel,
        in_specs=[pl.BlockSpec(memory_space=pltpu.SMEM)]
        + [pl.BlockSpec(memory_space=pltpu.VMEM)] * len(offers),
        out_specs=pl.BlockSpec(memory_space=pltpu.VMEM),
        out_shape=jax.ShapeDtypeStruct(offers[0].shape, offers[0].dtype),
        compiler_params=pltpu.CompilerParams(vmem_limit_bytes=VMEM),
        name="choose",
    )(info, *offers)


def shards(
    queries, key_rows, value_rows, frame_ids, ctx_keys, ctx_values, owners, ctx_lengths, out_weight
):
    rows, feat = queries.shape
    blk_count = lax.axis_size("blk")
    head_devices = lax.axis_size("heads")
    plane, pair = 4, 2
    depth, ring_y = blk_count // plane, head_devices // pair
    me = lax.axis_index("blk")
    head_me = lax.axis_index("heads")
    info = jnp.concatenate([owners, ctx_lengths, me[None], head_me[None]]).astype(jnp.int32)
    columns = [[c + plane * z for z in range(depth)] for c in range(plane)]

    def shift(item, distance):
        steps = [(i, (i + plane * distance) % blk_count) for i in range(blk_count)]
        return lax.ppermute(item, "blk", steps)

    def swap(item, mask):
        return lax.ppermute(item, "blk", [(i, i ^ mask) for i in range(blk_count)])

    def shift_y(item, step):
        steps = [(i, (i + pair * step) % head_devices) for i in range(head_devices)]
        return lax.ppermute(item, "heads", steps)

    marks = jnp.pad(frame_ids.astype(jnp.bfloat16)[None], ((0, 15), (0, 2 * feat - rows)))
    mid = rows // 2
    part = ctx_keys.shape[1] // depth
    both = jnp.concatenate([key_rows, value_rows], axis=1)
    own = jnp.concatenate([both[:mid], jnp.zeros((part, 2 * feat), both.dtype), both[mid:], marks])
    query_own = jnp.concatenate([queries.T, marks[:, :rows]], axis=0)
    slot = jnp.concatenate([ctx_keys[0], ctx_values[0]], axis=1).reshape(depth, part, 2 * feat)

    ahead, behind = shift(own, 1), shift(own, -1)
    query_x, query_core = swap(query_own, 2), swap(query_own, 1)
    pieces = lax.all_to_all(slot, "blk", 0, 0, axis_index_groups=columns)
    slabs = column_blocks(out_weight, info, feat, ring_y)
    pieces, query_x, query_core, *slabs = lax.optimization_barrier(
        (pieces, query_x, query_core, *slabs)
    )
    offers = list(offer_pieces(pieces, info))
    offers = offers[:1] + [swap(offers[mask], mask) for mask in range(1, plane)]
    piece = choose_piece(offers, info)

    def loaded(item):
        return lax.dynamic_update_slice(item, piece, (mid, 0))

    def halves(item):
        return [(item, 0, mid), (item, mid + part, mid)], item

    def carried(item):
        return item, mid, part

    slab_own, slab_core = slabs[0], slabs[ring_y]
    *first, query_x, query_core, slab_near, slab_far, slab_back = lax.optimization_barrier(
        (loaded(ahead), loaded(behind), query_x, query_core, *slabs[1:ring_y])
    )
    query_both = swap(query_x, 1)
    query_plane = jnp.concatenate([query_x, query_both, query_own, query_core], axis=1)
    ahead, behind = shift(first[0], 1), shift(first[1], -1)
    *state, token = attention_call(
        query_plane, [halves(item) for item in (own, *first)], None, None, False, info
    )
    slab_near = shift_y(slab_near, 1)
    slab_back = shift_y(slab_back, ring_y - 1)
    slab_far = shift_y(slab_far, 2)

    *second, token = lax.optimization_barrier((ahead, behind, token))
    ahead, behind = shift(second[0], 1), shift(second[1], -1)
    *state, token = attention_call(
        query_plane, [halves(item) for item in second], state, None, False, token
    )
    ahead, behind, slab_near, slab_back, slab_far, token = lax.optimization_barrier(
        (ahead, behind, slab_near, slab_back, slab_far, token)
    )

    far_ahead, far_behind = shift(ahead[: mid + part], 1), shift(behind[mid:], -1)
    opposite = shift(ahead[mid : mid + part], 2)
    *state, token = attention_call(
        query_plane, [halves(ahead), halves(behind)], state, None, False, token
    )
    far = [(far_ahead, 0, mid), (far_behind, part, mid)], far_behind
    ctx = [
        (far_ahead, mid, part),
        carried(ahead),
        carried(second[0]),
        (piece, 0, part),
        carried(second[1]),
        carried(behind),
        (far_behind, 0, part),
        (opposite, 0, part),
    ]
    finish = [far, (ctx, None)]
    keep, send = attention_call(query_plane, finish, state, info, True, token, 0)
    other = merge_call([keep, swap(send, 1)], False)
    other, token = lax.optimization_barrier((other, token))
    keep, send = attention_call(query_plane, finish, state, info, True, token, 1)
    own_slabs = [slab_own, slab_near, slab_far, slab_back]
    core_slabs = [slab_core] + [swap(item, 1) for item in own_slabs[1:]]
    received, *core_slabs = lax.optimization_barrier((swap(other, 2), *core_slabs))
    own = merge_call([keep, received], False)
    attended = merge_call([own, swap(send, 1)], True)

    def dots(block, step):
        return [
            jnp.dot(block, item[step], preferred_element_type=jnp.float32)
            for item in (own_slabs, core_slabs)
        ]

    total = dots(attended, 0)
    blocks = [(shift_y(attended, step), step) for step in (1, ring_y - 1, 2)]
    same = jnp.bitwise_and(jnp.bitwise_xor(me, head_me), 1) == 0
    *blocks, (block_far, step_far) = blocks
    for block, step in blocks:
        block, *total = lax.optimization_barrier((block, *total))
        total = [old + new for old, new in zip(total, dots(block, step))]
    pairs = [total, (own_slabs[step_far], core_slabs[step_far])]
    pairs = [(jnp.where(same, b, a), jnp.where(same, a, b)) for a, b in pairs]
    (other, mine), (slab_other, slab_mine) = pairs
    block_far, other, mine, slab_other, slab_mine = lax.optimization_barrier(
        (block_far, other, mine, slab_other, slab_mine)
    )
    other += jnp.dot(block_far, slab_other, preferred_element_type=jnp.float32)
    mine += jnp.dot(block_far, slab_mine, preferred_element_type=jnp.float32)
    received = lax.ppermute(
        other.astype(jnp.bfloat16), "heads", [(i, i ^ 1) for i in range(head_devices)]
    )
    return (mine + received.astype(jnp.float32)).astype(jnp.bfloat16)


def solution(mesh):
    return jax.shard_map(
        shards,
        mesh=mesh,
        in_specs=(
            P("blk", "heads"),
            P("blk", "heads"),
            P("blk", "heads"),
            P("blk"),
            P("blk", None, "heads"),
            P("blk", None, "heads"),
            P(),
            P(),
            P("heads", None),
        ),
        out_specs=P("blk", "heads"),
        check_vma=False,
    )
```

```python
import functools
import math

import jax
import jax.numpy as jnp
from jax import lax
from jax.experimental import pallas as pl
from jax.experimental.pallas import tpu as pltpu
from jax.sharding import PartitionSpec as P

DH = 128
LOW = -1e30
MASKED = -3e30
FRAMES = 8
VMEM = 60 << 20


def scaled_exponent():
    return DH ** (-0.5) * math.log2(math.e)


def attention_kernel(array_count, layout, first, last, with_ctx, head_count, rows, *refs):
    refs = list(refs)
    ctx_info = refs.pop(0) if with_ctx else None
    refs.pop(0)
    query_ref = refs.pop(0)
    query_marks = refs.pop(0)
    arrays = [refs.pop(0) for _ in range(array_count)]
    chunk_count = len(layout)
    if not first:
        acc_in = refs.pop(0)
        stat_in = refs.pop(0)
    if last:
        keep_out = refs.pop(0)
        send_out = refs.pop(0)
    else:
        acc_out = refs.pop(0)
        stat_out = refs.pop(0)
        token_out = refs.pop(0)
    limits = refs.pop(0)
    bounds = refs.pop(0)
    if last:
        stats = refs.pop(0)

    step = pl.program_id(0)
    heads = range(head_count) if last else [step]
    span = query_ref.shape[1]
    lane = 128
    factor = scaled_exponent()

    @pl.when(step == 0)
    def _():
        for index, (_, mark) in enumerate(layout):
            if mark is None:
                live = ctx_info[4 + jnp.bitwise_and(ctx_info[8], 3)]
                limits[index, 0:1, :] = jnp.full(
                    (1, span), live.astype(jnp.float32), jnp.float32
                )
                bounds[index] = jnp.int32(1)
                continue
            frame = lax.broadcasted_iota(jnp.int32, (FRAMES, rows), 0).astype(jnp.float32)
            marks_at, mark_row = mark
            key_marks = arrays[marks_at][mark_row : mark_row + 16, 0:rows][0:1].astype(jnp.float32)
            below = jnp.sum((key_marks <= frame).astype(jnp.float32), axis=1, keepdims=True)
            frame = lax.broadcasted_iota(jnp.int32, (FRAMES, span), 0).astype(jnp.float32)
            marks = query_marks[0:1, :].astype(jnp.float32)
            most = jnp.sum(jnp.where(marks == frame, below, 0.0), axis=0, keepdims=True)
            limits[index, 0:1, :] = most
            bounds[index] = jnp.max(most).astype(jnp.int32)

    def update(head, at):
        query_rows, stat_rows = slice(at * DH, (at + 1) * DH), at * 8
        row = lax.broadcasted_iota(jnp.int32, (rows, lane), 0)
        places = [row.astype(jnp.float32)] * chunk_count
        if with_ctx:
            start = (lax.shift_right_logical(ctx_info[8], 2) + 5) * (rows // 8)
            places[-1] = jnp.bitwise_and(row + start, rows - 1).astype(jnp.float32)

        def joined(segments, column):
            begin_lane = (column + head) * DH
            if not last:
                begin_lane = pl.multiple_of(begin_lane, DH)
            lanes = pl.ds(begin_lane, DH)
            return jnp.concatenate(
                [arrays[which][begin : begin + count, lanes] for which, begin, count in segments]
            )

        keys = [joined(segments, 0) for segments, _ in layout]
        turned = [joined(segments, head_count).T for segments, _ in layout]
        for tile in range(span // lane):
            spot = slice(tile * lane, (tile + 1) * lane)
            query = query_ref[query_rows, spot]
            if first:
                top = jnp.full((1, lane), LOW, jnp.float32)
                total = jnp.zeros((1, lane), jnp.float32)
                acc = jnp.zeros((DH, lane), jnp.float32)
            else:
                top = stat_in[stat_rows : stat_rows + 1, spot]
                total = stat_in[stat_rows + 1 : stat_rows + 2, spot]
                acc = acc_in[query_rows, spot]
            for index in range(chunk_count):
                scores = jnp.dot(keys[index], query, preferred_element_type=jnp.float32)
                scores = jnp.where(places[index] < limits[index, 0:1, spot], scores, MASKED)
                top_new = jnp.maximum(top, jnp.max(scores, axis=0, keepdims=True))
                weights = jnp.exp2((scores - top_new) * factor)
                fade = jnp.exp2((top - top_new) * factor)
                total = total * fade + jnp.sum(weights, axis=0, keepdims=True)
                acc = acc * fade + jnp.dot(
                    turned[index],
                    weights.astype(jnp.bfloat16),
                    preferred_element_type=jnp.float32,
                )
                top = top_new
            if not last:
                stat_out[0:1, spot] = top
                stat_out[1:2, spot] = total
                acc_out[:, spot] = acc
                continue
            out_ref, begin = (keep_out, 0) if tile * lane < rows else (send_out, rows)
            out_spot = slice(tile * lane - begin, (tile + 1) * lane - begin)
            out_ref[query_rows, out_spot] = (acc * (1.0 / total)).astype(jnp.bfloat16)
            level = top * factor + jnp.log2(total)
            for part in range(3):
                piece = level.astype(jnp.bfloat16).astype(jnp.float32)
                stats[part * head_count + head : part * head_count + head + 1, spot] = piece
                level = level - piece

    if first or last:
        for at, head in enumerate(heads):
            update(head, at)
    else:
        seen = functools.reduce(jnp.maximum, [bounds[index] for index in range(chunk_count)]) > 0

        @pl.when(seen)
        def _():
            update(step, 0)

        @pl.when(jnp.logical_not(seen))
        def _():
            acc_out[...] = acc_in[...]
            stat_out[0:2, :] = stat_in[0:2, :]

    if not last:
        token_out[...] = jnp.zeros_like(token_out)
    else:
        feat = head_count * DH
        keep_out[feat : feat + 16, :] = stats[:, :rows].astype(jnp.bfloat16)
        send_out[feat : feat + 16, :] = stats[:, rows:].astype(jnp.bfloat16)


def attention_call(queries, chunks, state, ctx_info, last, token, side=0):
    feat = queries.shape[0] - 16
    rows = queries.shape[1] // 4
    head_count = feat // DH
    first = state is None
    span = (2 if last else 4) * rows
    steps = 1 if last else head_count
    high = head_count // steps
    with_ctx = ctx_info is not None
    operands, specs = [], []
    if with_ctx:
        operands.append(ctx_info)
        specs.append(pl.BlockSpec(memory_space=pltpu.SMEM))
    operands += [token, queries, queries]
    specs.append(pl.BlockSpec(memory_space=pl.ANY))
    specs.append(pl.BlockSpec((high * DH, span), lambda h: (h, side)))
    specs.append(pl.BlockSpec((16, span), lambda h: (feat // 16, side)))
    found = []
    for segments, _ in chunks:
        for array, begin, count in segments:
            for known, places in found:
                if known is array:
                    places.add((begin, count))
                    break
            else:
                found.append((array, {(begin, count)}))
    starts = []
    for array, places in found:
        begin, count = min(places)
        exact = len(places) == 1 and begin % count == 0
        operands.append(array)
        shape = (count if exact else array.shape[0], array.shape[1])
        at = begin // count if exact else 0
        specs.append(pl.BlockSpec(shape, lambda h, at=at: (at, 0)))
        starts.append(begin if exact else 0)

    def number(array):
        return next(at for at, (known, _) in enumerate(found) if known is array)

    layout = []
    for segments, marks in chunks:
        parts = tuple(
            (number(array), begin - starts[number(array)], count)
            for array, begin, count in segments
        )
        layout.append((parts, None if marks is None else (number(marks), marks.shape[0] - 16)))
    aliases = {}
    state_specs = [
        pl.BlockSpec((high * DH, span), lambda h: (h, side)),
        pl.BlockSpec((high * 8, span), lambda h: (h, side)),
    ]
    if not first:
        if not last:
            aliases = {len(operands): 0, len(operands) + 1: 1}
        operands.extend(state)
        specs.extend(state_specs)
    if last:
        out_shape = [jax.ShapeDtypeStruct((feat + 16, rows), jnp.bfloat16)] * 2
        out_specs = [pl.BlockSpec((feat + 16, rows), lambda h: (0, 0))] * 2
    else:
        out_shape = [
            jax.ShapeDtypeStruct((feat, span), jnp.float32),
            jax.ShapeDtypeStruct((8 * head_count, span), jnp.float32),
            jax.ShapeDtypeStruct((8, 128), jnp.float32),
        ]
        out_specs = state_specs + [pl.BlockSpec((8, 128), lambda h: (0, 0))]
    scratch = [
        pltpu.VMEM((len(chunks), 8, span), jnp.float32),
        pltpu.SMEM((len(chunks),), jnp.int32),
    ]
    if last:
        scratch.append(pltpu.VMEM((16, span), jnp.float32))
    return pl.pallas_call(
        functools.partial(
            attention_kernel, len(found), layout, first, last, with_ctx, head_count, rows
        ),
        grid=(steps,),
        in_specs=specs,
        out_specs=out_specs,
        out_shape=out_shape,
        scratch_shapes=scratch,
        input_output_aliases=aliases,
        cost_estimate=pl.CostEstimate(
            flops=len(chunks) * span * 6 * 10**6, bytes_accessed=8 << 20, transcendentals=0
        ),
        compiler_params=pltpu.CompilerParams(vmem_limit_bytes=VMEM),
        name="attend",
    )(*operands)


def merge_kernel(head_count, turned, *refs):
    *in_refs, out_ref = refs
    feat = head_count * DH
    rows = in_refs[0].shape[1]
    stats = [ref[feat : feat + 16, :].astype(jnp.float32) for ref in in_refs]
    pieces = [[], [], []]
    for head in range(head_count):
        levels = [
            s[head : head + 1]
            + s[head_count + head : head_count + head + 1]
            + s[2 * head_count + head : 2 * head_count + head + 1]
            for s in stats
        ]
        top = functools.reduce(jnp.maximum, levels)
        shares = [jnp.exp2(level - top) for level in levels]
        total = sum(shares)
        inverse = 1.0 / total
        span = slice(head * DH, (head + 1) * DH)
        mixed = sum(
            ref[span, :].astype(jnp.float32) * (share * inverse)
            for ref, share in zip(in_refs, shares)
        )
        if turned:
            out_ref[:, span] = mixed.T.astype(jnp.bfloat16)
        else:
            out_ref[span, :] = mixed.astype(jnp.bfloat16)
            level = top + jnp.log2(total)
            for part in range(3):
                piece = level.astype(jnp.bfloat16).astype(jnp.float32)
                pieces[part].append(piece)
                level = level - piece
    if not turned:
        out_ref[feat : feat + 16, :] = jnp.concatenate(
            pieces[0] + pieces[1] + pieces[2] + [jnp.zeros((1, rows), jnp.float32)], axis=0
        ).astype(jnp.bfloat16)


def merge_call(parts, turned):
    feat = parts[0].shape[0] - 16
    rows = parts[0].shape[1]
    shape = (rows, feat) if turned else (feat + 16, rows)
    return pl.pallas_call(
        functools.partial(merge_kernel, feat // DH, turned),
        in_specs=[pl.BlockSpec(memory_space=pltpu.VMEM)] * len(parts),
        out_specs=pl.BlockSpec(memory_space=pltpu.VMEM),
        out_shape=jax.ShapeDtypeStruct(shape, jnp.bfloat16),
        compiler_params=pltpu.CompilerParams(vmem_limit_bytes=VMEM),
        cost_estimate=pl.CostEstimate(flops=0, bytes_accessed=1 << 10, transcendentals=0),
        name="merge",
    )(*parts)


def columns_kernel(ring, info, in_ref, *out_refs):
    width = out_refs[0].shape[1]
    core = jnp.bitwise_and(info[8], 1)
    for step, out_ref in enumerate(out_refs):
        target = jnp.bitwise_and(lax.shift_right_logical(info[9], 1) + step, ring - 1)
        half = core if step < ring else 1 - core
        begin = pl.multiple_of((2 * target + half) * width, DH)
        out_ref[...] = in_ref[:, pl.ds(begin, width)]


def column_blocks(weight, info, width, ring):
    rows, total = weight.shape
    return pl.pallas_call(
        functools.partial(columns_kernel, ring),
        grid=(rows // DH,),
        in_specs=[
            pl.BlockSpec(memory_space=pltpu.SMEM),
            pl.BlockSpec((DH, total), lambda i: (i, 0)),
        ],
        out_specs=[pl.BlockSpec((DH, width), lambda i: (i, 0))] * (ring + 1),
        out_shape=[jax.ShapeDtypeStruct((rows, width), weight.dtype)] * (ring + 1),
        compiler_params=pltpu.CompilerParams(vmem_limit_bytes=VMEM),
        cost_estimate=pl.CostEstimate(
            flops=0, bytes_accessed=4 * (ring + 1) * rows * width, transcendentals=0
        ),
        name="columns",
    )(info, weight)


def offer_kernel(info, in_ref, *out_refs):
    for mask, out_ref in enumerate(out_refs):
        owner = info[jnp.bitwise_xor(jnp.bitwise_and(info[8], 3), mask)]
        out_ref[...] = in_ref[lax.shift_right_logical(owner, 2)]


def offer_pieces(pieces, info):
    return pl.pallas_call(
        offer_kernel,
        in_specs=[
            pl.BlockSpec(memory_space=pltpu.SMEM),
            pl.BlockSpec(memory_space=pltpu.VMEM),
        ],
        out_specs=[pl.BlockSpec(memory_space=pltpu.VMEM)] * 4,
        out_shape=[jax.ShapeDtypeStruct(pieces.shape[1:], pieces.dtype)] * 4,
        compiler_params=pltpu.CompilerParams(vmem_limit_bytes=VMEM),
        name="offer",
    )(info, pieces)


def choose_kernel(info, *refs):
    kind = jnp.bitwise_and(info[8], 3)
    source = jnp.bitwise_xor(jnp.bitwise_and(info[kind], 3), kind)
    out_ref = refs[-1]
    for mask, in_ref in enumerate(refs[:-1]):

        @pl.when(source == mask)
        def _(in_ref=in_ref):
            out_ref[...] = in_ref[...]


def choose_piece(offers, info):
    return pl.pallas_call(
        choose_kernel,
        in_specs=[pl.BlockSpec(memory_space=pltpu.SMEM)]
        + [pl.BlockSpec(memory_space=pltpu.VMEM)] * len(offers),
        out_specs=pl.BlockSpec(memory_space=pltpu.VMEM),
        out_shape=jax.ShapeDtypeStruct(offers[0].shape, offers[0].dtype),
        compiler_params=pltpu.CompilerParams(vmem_limit_bytes=VMEM),
        name="choose",
    )(info, *offers)


def shards(
    queries, key_rows, value_rows, frame_ids, ctx_keys, ctx_values, owners, ctx_lengths, out_weight
):
    rows, feat = queries.shape
    blk_count = lax.axis_size("blk")
    head_devices = lax.axis_size("heads")
    plane, pair = 4, 2
    depth, ring_y = blk_count // plane, head_devices // pair
    me = lax.axis_index("blk")
    head_me = lax.axis_index("heads")
    info = jnp.concatenate([owners, ctx_lengths, me[None], head_me[None]]).astype(jnp.int32)
    columns = [[c + plane * z for z in range(depth)] for c in range(plane)]

    def shift(item, distance):
        steps = [(i, (i + plane * distance) % blk_count) for i in range(blk_count)]
        return lax.ppermute(item, "blk", steps)

    def swap(item, mask):
        return lax.ppermute(item, "blk", [(i, i ^ mask) for i in range(blk_count)])

    def shift_y(item, step):
        steps = [(i, (i + pair * step) % head_devices) for i in range(head_devices)]
        return lax.ppermute(item, "heads", steps)

    marks = jnp.pad(frame_ids.astype(jnp.bfloat16)[None], ((0, 15), (0, 2 * feat - rows)))
    mid = 3 * rows // 8
    part = ctx_keys.shape[1] // depth
    both = jnp.concatenate([key_rows, value_rows], axis=1)
    own = jnp.concatenate([both[:mid], jnp.zeros((part, 2 * feat), both.dtype), both[mid:], marks])
    query_own = jnp.concatenate([queries.T, marks[:, :rows]], axis=0)
    slot = jnp.concatenate([ctx_keys[0], ctx_values[0]], axis=1).reshape(depth, part, 2 * feat)

    ahead, behind = shift(own, 1), shift(own, -1)
    query_x, query_core = swap(query_own, 2), swap(query_own, 1)
    pieces = lax.all_to_all(slot, "blk", 0, 0, axis_index_groups=columns)
    slabs = column_blocks(out_weight, info, feat, ring_y)
    pieces, query_x, query_core, *slabs = lax.optimization_barrier(
        (pieces, query_x, query_core, *slabs)
    )
    offers = list(offer_pieces(pieces, info))
    offers = offers[:1] + [swap(offers[mask], mask) for mask in range(1, plane)]
    piece = choose_piece(offers, info)

    def loaded(item):
        return lax.dynamic_update_slice(item, piece, (mid, 0))

    def halves(item):
        return [(item, 0, mid), (item, mid + part, rows - mid)], item

    def carried(item):
        return item, mid, part

    slab_own, slab_core = slabs[0], slabs[ring_y]
    *first, query_x, query_core, slab_near, slab_far, slab_back = lax.optimization_barrier(
        (loaded(ahead), loaded(behind), query_x, query_core, *slabs[1:ring_y])
    )
    query_both = swap(query_x, 1)
    query_plane = jnp.concatenate([query_x, query_both, query_own, query_core], axis=1)
    ahead, behind = shift(first[0], 1), shift(first[1], -1)
    *state, token = attention_call(
        query_plane, [halves(item) for item in (own, *first)], None, None, False, info
    )
    slab_near = shift_y(slab_near, 1)
    slab_back = shift_y(slab_back, ring_y - 1)
    slab_far = shift_y(slab_far, 2)

    *second, token = lax.optimization_barrier((ahead, behind, token))
    ahead, behind = shift(second[0], 1), shift(second[1], -1)
    *state, token = attention_call(
        query_plane, [halves(item) for item in second], state, None, False, token
    )
    ahead, behind, slab_near, slab_back, slab_far, token = lax.optimization_barrier(
        (ahead, behind, slab_near, slab_back, slab_far, token)
    )

    far_ahead, far_behind = shift(ahead[: mid + part], 1), shift(behind[mid:], -1)
    opposite = shift(ahead[mid : mid + part], 2)
    *state, token = attention_call(
        query_plane, [halves(ahead), halves(behind)], state, None, False, token
    )
    far = [(far_ahead, 0, mid), (far_behind, part, rows - mid)], far_behind
    ctx = [
        (far_ahead, mid, part),
        carried(ahead),
        carried(second[0]),
        (piece, 0, part),
        carried(second[1]),
        carried(behind),
        (far_behind, 0, part),
        (opposite, 0, part),
    ]
    finish = [far, (ctx, None)]
    keep, send = attention_call(query_plane, finish, state, info, True, token, 0)
    other = merge_call([keep, swap(send, 1)], False)
    other, token = lax.optimization_barrier((other, token))
    keep, send = attention_call(query_plane, finish, state, info, True, token, 1)
    own_slabs = [slab_own, slab_near, slab_far, slab_back]
    core_slabs = [slab_core] + [swap(item, 1) for item in own_slabs[1:]]
    received, *core_slabs = lax.optimization_barrier((swap(other, 2), *core_slabs))
    own = merge_call([keep, received], False)
    attended = merge_call([own, swap(send, 1)], True)

    def dots(block, step):
        return [
            jnp.dot(block, item[step], preferred_element_type=jnp.float32)
            for item in (own_slabs, core_slabs)
        ]

    total = dots(attended, 0)
    blocks = [(shift_y(attended, step), step) for step in (1, ring_y - 1, 2)]
    same = jnp.bitwise_and(jnp.bitwise_xor(me, head_me), 1) == 0
    *blocks, (block_far, step_far) = blocks
    for block, step in blocks:
        block, *total = lax.optimization_barrier((block, *total))
        total = [old + new for old, new in zip(total, dots(block, step))]
    pairs = [total, (own_slabs[step_far], core_slabs[step_far])]
    pairs = [(jnp.where(same, b, a), jnp.where(same, a, b)) for a, b in pairs]
    (other, mine), (slab_other, slab_mine) = pairs
    block_far, other, mine, slab_other, slab_mine = lax.optimization_barrier(
        (block_far, other, mine, slab_other, slab_mine)
    )
    other += jnp.dot(block_far, slab_other, preferred_element_type=jnp.float32)
    mine += jnp.dot(block_far, slab_mine, preferred_element_type=jnp.float32)
    received = lax.ppermute(
        other.astype(jnp.bfloat16), "heads", [(i, i ^ 1) for i in range(head_devices)]
    )
    return (mine + received.astype(jnp.float32)).astype(jnp.bfloat16)


def solution(mesh):
    return jax.shard_map(
        shards,
        mesh=mesh,
        in_specs=(
            P("blk", "heads"),
            P("blk", "heads"),
            P("blk", "heads"),
            P("blk"),
            P("blk", None, "heads"),
            P("blk", None, "heads"),
            P(),
            P(),
            P("heads", None),
        ),
        out_specs=P("blk", "heads"),
        check_vma=False,
    )
```
